512 devices in a mesh: fourier: 16 (over x_hi, y, core), meridian: 32 (over z, x_lo).
Axes of the slice: x: 4 (x_hi: 2, x_lo: 2; x = x_hi * 2 + x_lo), y: 4, z: 16, core: 2. Of those that a mesh axis runs over, the one named last changes fastest.
Arguments:
- forward_now: float32 [3, 4224, 2048], P(None, 'meridian', 'fourier'), may hold values from -3 to 3
- forward_last: float32 [3, 4224, 2048], P(None, 'meridian', 'fourier'), may hold values from -3 to 3
- adjoint_now: float32 [3, 4224, 2048], P(None, 'meridian', 'fourier'), may hold values from -3 to 3
- adjoint_last: float32 [3, 4224, 2048], P(None, 'meridian', 'fourier'), may hold values from -3 to 3
- moduli: float32 [21, 17, 32, 400], P(None, None, 'meridian', 'fourier'), may hold values from -1.8 to 1.8
- inv_radius: float32 [12800], P('meridian'), may hold values from 0.0009765625 to 0.0078125
- inv_mass: float32 [8448], P('meridian'), may hold values from 0.005 to 0.05
Outputs:
- forward_next: float32 [3, 4224, 2048], P(None, 'meridian', 'fourier')
- adjoint_next: float32 [3, 4224, 2048], P(None, 'meridian', 'fourier')
- kernel: float32 [21, 17, 32, 400], P(None, None, 'meridian', 'fourier')
The draws below stay inside these ranges and needn't reach their ends.
All inputs are finite; a program needn't handle non-finite values.
Results may differ from the reference program's by a relative error of at most 0.0001.
Values sent between devices are 32-bit elements; how exact they have to be, the bound alone decides.
No kernel may reach another device: no remote copies, remote signals or barrier semaphores. Data moves between devices by JAX's collectives and lax.ppermute only.
A program may use at most 64 MiB of HBM per device.

```python
import math
import jax
import jax.numpy as jnp
import numpy as np
from jax import lax

F = 1024
ORD = 8
EB = 8
EA = 2
BASIS = 17
SLICES = 32
NPTS = 8448
Q = 400
NQ = 12800
N_MERIDIAN = 32


def block_levels(stream_key, dims, pieces, least, top_value):
    loudness, own = 1.0, jax.random.fold_in(stream_key, 6)
    for axis_at, parts in pieces:
        draws = jnp.exp(jax.random.uniform(jax.random.fold_in(own, axis_at), (parts,), jnp.float32, least / len(pieces), top_value / len(pieces)))
        loudness = loudness * jnp.repeat(draws, dims[axis_at] // parts).reshape([-1 if axis == axis_at else 1 for axis in range(len(dims))])
    return loudness


def normal_values(own_key, shape, spread, reach, shards=(), kind=jnp.bfloat16):
    gain = block_levels(own_key, shape, shards, -0.22, 0.18) if shards else 1.0
    drawn = jax.random.normal(own_key, shape, jnp.float32) * spread * gain
    return jnp.minimum(jnp.maximum(drawn, -reach), reach).astype(kind)


def setup_inputs(seed: int = 0) -> dict:
    key_of = jax.random.split(jax.random.key(seed), 8)
    forward_now = normal_values(key_of[0], (3, NPTS // 2, 2 * F), 0.5, 3.0, ((1, 32), (2, 16)), jnp.float32)
    forward_last = normal_values(key_of[1], (3, NPTS // 2, 2 * F), 0.5, 3.0, ((1, 32), (2, 16)), jnp.float32)
    adjoint_now = normal_values(key_of[2], (3, NPTS // 2, 2 * F), 0.5, 3.0, ((1, 32), (2, 16)), jnp.float32)
    adjoint_last = normal_values(key_of[3], (3, NPTS // 2, 2 * F), 0.5, 3.0, ((1, 32), (2, 16)), jnp.float32)
    moduli = normal_values(key_of[4], (21, BASIS, SLICES, Q), 0.3, 1.8, ((2, 32), (3, 16)), jnp.float32)
    inv_radius = jnp.clip(jnp.exp(math.log(0.0078125) - 2.0794415 * jax.random.uniform(key_of[5], (NQ,), jnp.float32) ** block_levels(key_of[5], (NQ,), ((0, 32),), -0.2, 0.2)), 0.0009765625, 0.0078125)
    inv_mass = jnp.clip(jnp.exp(math.log(0.05) - 2.3025851 * jax.random.uniform(key_of[6], (NPTS,), jnp.float32) ** block_levels(key_of[6], (NPTS,), ((0, 32),), -0.2, 0.2)), 0.005, 0.05)
    return {"forward_now": forward_now, "forward_last": forward_last, "adjoint_now": adjoint_now, "adjoint_last": adjoint_last, "moduli": moduli, "inv_radius": inv_radius, "inv_mass": inv_mass}


highest = lax.Precision.HIGHEST
kernel_weight = 0.0001

def unpack_points(values):
    shape = values.shape
    evens = values[:, :, 0::2]
    odds = values[:, :, 1::2]
    return jnp.stack([evens, odds], axis=2).reshape(shape[0], 2 * shape[1], shape[2] // 2)

def pack_points(values):
    shape = values.shape
    paired = values.reshape(shape[0], shape[1] // 2, 2, shape[2])
    packed = jnp.zeros((shape[0], shape[1] // 2, 2 * shape[2]), values.dtype)
    packed = packed.at[:, :, 0::2].set(paired[:, :, 0])
    return packed.at[:, :, 1::2].set(paired[:, :, 1])

def gll_tables():
    points_x = np.array([-1.0, -math.sqrt(3.0 / 7.0), 0.0, math.sqrt(3.0 / 7.0), 1.0])
    weights = np.array([0.1, 49.0 / 90.0, 32.0 / 45.0, 49.0 / 90.0, 0.1])
    factor = np.array([np.prod([points_x[row_at] - points_x[column] for column in range(5) if column != row_at]) for row_at in range(5)])
    derive = np.zeros((5, 5))
    for row_at in range(5):
        for col_at in range(5):
            if row_at != col_at:
                derive[row_at, col_at] = factor[row_at] / (factor[col_at] * (points_x[row_at] - points_x[col_at]))
            else:
                derive[row_at, col_at] = sum((1.0 / (points_x[row_at] - points_x[column]) for column in range(5) if column != row_at))
    return (jnp.asarray(derive, jnp.float32), jnp.asarray(np.outer(weights, weights).reshape(25), jnp.float32))

def sample_table(count):
    sample_ids = jnp.arange(count, dtype=jnp.int32)
    orders = jnp.where(sample_ids == 1, count // 2, sample_ids // 2).astype(jnp.int32)
    phases = sample_ids[:, None] * orders[None, :] % count
    angles = phases.astype(jnp.float32) * (2.0 * math.pi / count)
    sine_cols = (sample_ids % 2 == 1) & (sample_ids != 1)
    return jnp.where(sine_cols[None, :], jnp.sin(angles), jnp.cos(angles))

def basis_table(count, degree):
    sample_ids = jnp.arange(count, dtype=jnp.int32)
    column = jnp.arange(2 * degree + 1, dtype=jnp.int32)
    orders = (column + 1) // 2
    phases = sample_ids[:, None] * orders[None, :] % count
    angles = phases.astype(jnp.float32) * (2.0 * math.pi / count)
    sine_cols = (column % 2 == 0) & (column > 0)
    return jnp.where(sine_cols[None, :], jnp.sin(angles), jnp.cos(angles))

def node_weights(weights, count):
    return jnp.tile(weights, count // 25)

def to_blocks(values, count):
    width = values.shape[-1]
    leading = values[..., :4 * count, :].reshape(values.shape[:-2] + (count, 4, width))
    closing = values[..., 4::4, :][..., None, :]
    return jnp.concatenate([leading, closing], axis=-2)

def from_blocks(blocks, count):
    width = blocks.shape[-1]
    outer = blocks.shape[:-3]
    edge_pad = [(0, 0)] * len(outer)
    leading = blocks[..., :4, :].reshape(outer + (4 * count, width))
    leading = jnp.pad(leading, edge_pad + [(0, 1), (0, 0)])
    closing = jnp.pad(blocks[..., 4:, :], edge_pad + [(0, 0), (3, 0), (0, 0)])
    closing = jnp.pad(closing.reshape(outer + (4 * count, width)), edge_pad + [(1, 0), (0, 0)])
    return leading + closing

def to_elements(field, count_a, count_b):
    leads = field.shape[0]
    width = field.shape[-1]
    columns = to_blocks(field, count_b)
    columns = jnp.transpose(columns, (0, 2, 3, 1, 4))
    grid_blocks = to_blocks(columns, count_a)
    grid_blocks = jnp.transpose(grid_blocks, (0, 3, 1, 4, 2, 5))
    return grid_blocks.reshape(leads, count_a * count_b, 5, 5, width)

def from_elements(elements, count_a, count_b):
    leads = elements.shape[0]
    width = elements.shape[-1]
    grid_blocks = elements.reshape(leads, count_a, count_b, 5, 5, width)
    grid_blocks = jnp.transpose(grid_blocks, (0, 2, 4, 1, 3, 5))
    row_sums = from_blocks(grid_blocks, count_a)
    row_sums = jnp.transpose(row_sums, (0, 3, 1, 2, 4))
    return from_blocks(row_sums, count_b)

def azimuth(values, orders):
    orders_each = jnp.repeat(orders, 2)
    positions = jnp.arange(values.shape[-1], dtype=jnp.int32)
    is_even = positions % 2 == 0
    following = jnp.roll(values, -1, axis=-1)
    preceding = jnp.roll(values, 1, axis=-1)
    return jnp.where(is_even, orders_each * following, -orders_each * preceding)

def strains(displace, radius, orders, derive):
    along_a = jnp.einsum('ik,lcekjn->lceijn', derive, displace, precision=highest)
    along_b = jnp.einsum('jk,lceikn->lceijn', derive, displace, precision=highest)
    beside_all = radius[..., None] * azimuth(displace, orders)
    return jnp.stack([along_a[:, 0], along_b[:, 1], beside_all[:, 2], along_b[:, 2] + beside_all[:, 1], along_a[:, 2] + beside_all[:, 0], along_a[:, 1] + along_b[:, 0]], axis=1)

def forces(stress, radius, orders, derive):
    part_a = jnp.stack([stress[:, 0], stress[:, 5], stress[:, 4]], axis=1)
    part_b = jnp.stack([stress[:, 5], stress[:, 1], stress[:, 3]], axis=1)
    part_p = jnp.stack([stress[:, 4], stress[:, 3], stress[:, 2]], axis=1)
    from_a = jnp.einsum('ki,lcekjn->lceijn', derive, part_a, precision=highest)
    from_b = jnp.einsum('kj,lceikn->lceijn', derive, part_b, precision=highest)
    return from_a + from_b - azimuth(radius[..., None] * part_p, orders)

def voigt_index(left_at, right_at):
    lesser = min(left_at, right_at)
    larger = max(left_at, right_at)
    return lesser * 6 - lesser * (lesser - 1) // 2 + larger - lesser

def stress_samples(strain, moduli_s, dft_table, weights_q):
    sampled = jnp.dot(strain, dft_table.T, precision=highest)
    stress_list = []
    for left_at in range(6):
        total = moduli_s[voigt_index(left_at, 0)] * sampled[:, 0]
        for right_at in range(1, 6):
            total = total + moduli_s[voigt_index(left_at, right_at)] * sampled[:, right_at]
        stress_list.append(total)
    weighted = jnp.stack(stress_list, axis=1) * weights_q[:, None]
    coeffs = jnp.dot(weighted, dft_table, precision=highest) / dft_table.shape[0]
    return (coeffs, sampled)

def kernel_terms(sampled, basis_rows, weights_q):
    forward_s = sampled[0]
    adjoint_s = sampled[1]
    terms = []
    for left_at in range(6):
        for right_at in range(left_at, 6):
            if left_at == right_at:
                terms.append(forward_s[left_at] * adjoint_s[left_at])
            else:
                terms.append(forward_s[left_at] * adjoint_s[right_at] + forward_s[right_at] * adjoint_s[left_at])
    stacked = jnp.stack(terms) * weights_q[:, None]
    projected = jnp.dot(stacked, basis_rows, precision=highest)
    return jnp.transpose(projected, (0, 2, 1)) * kernel_weight

def reference(forward_now, forward_last, adjoint_now, adjoint_last, moduli, inv_radius, inv_mass):
    forward_now = unpack_points(forward_now)
    forward_last = unpack_points(forward_last)
    adjoint_now = unpack_points(adjoint_now)
    adjoint_last = unpack_points(adjoint_last)
    derive, weights = gll_tables()
    width_b = 4 * EB + 1
    row_count = 4 * EA
    nodes_slice = 25 * EA * EB
    fields = jnp.stack([forward_now, adjoint_now]).reshape(2, 3, row_count * N_MERIDIAN, width_b, F)
    padded = jnp.pad(fields, ((0, 0), (0, 0), (0, 1), (0, 0), (0, 0)))
    dft_table = sample_table(F)
    basis_rows = basis_table(F, ORD)
    orders_full = jnp.arange(F // 2, dtype=jnp.int32).astype(jnp.float32)
    weights_q = node_weights(weights, nodes_slice)

    def one_slice(slice_at):
        block = lax.dynamic_slice_in_dim(padded, slice_at * row_count, row_count + 1, axis=2)
        block = block.reshape(6, row_count + 1, width_b, F)
        elements = to_elements(block, EA, EB).reshape(2, 3, EA * EB, 5, 5, F)
        radius = lax.dynamic_slice_in_dim(inv_radius, slice_at * nodes_slice, nodes_slice).reshape(EA * EB, 5, 5)
        moduli_m = lax.dynamic_index_in_dim(moduli, slice_at, axis=2, keepdims=False)
        moduli_s = jnp.einsum('cjq,nj->cqn', moduli_m, basis_rows, precision=highest)
        strain = strains(elements, radius, orders_full, derive).reshape(2, 6, nodes_slice, F)
        coeffs, sampled = stress_samples(strain, moduli_s, dft_table, weights_q)
        pushed = forces(coeffs.reshape(2, 6, EA * EB, 5, 5, F), radius, orders_full, derive)
        assembled = from_elements(pushed.reshape(6, EA * EB, 5, 5, F), EA, EB)
        return (assembled, kernel_terms(sampled, basis_rows, weights_q))
    assembled, kernel = lax.map(one_slice, jnp.arange(N_MERIDIAN, dtype=jnp.int32))
    own_rows = assembled[:, :, :row_count]
    carried = jnp.concatenate([jnp.zeros_like(assembled[:1, :, row_count]), assembled[:-1, :, row_count]], axis=0)
    own_rows = own_rows.at[:, :, 0].add(carried)
    forces_all = jnp.transpose(own_rows, (1, 0, 2, 3, 4)).reshape(2, 3, NPTS, F)
    mass_scale = inv_mass[:, None]
    forward_next = 2.0 * forward_now - forward_last - mass_scale * forces_all[0]
    adjoint_next = 2.0 * adjoint_now - adjoint_last - mass_scale * forces_all[1]
    return (pack_points(forward_next), pack_points(adjoint_next), jnp.transpose(kernel, (1, 2, 0, 3)))
```

```python
import math

import jax
import jax.numpy as jnp
import ml_dtypes
import numpy as np
from jax import lax
from jax.experimental import pallas as pl
from jax.experimental.pallas import tpu as pltpu
from jax.sharding import PartitionSpec as P

FOURIER = "fourier"
MERIDIAN = "meridian"
PEERS = 16
OWN = 32
REACH = 8
LANES = 128
TOTAL = 1024
ROWS = 160
NEXT = 136
CHUNK = 40
PART = 80
NODES = 25

f32 = jnp.float32
bf16 = jnp.bfloat16


def wave_rows(f, order):
    if f == 0:
        low = 2.0 * np.pi * np.arange(96) / 96
        high = 2.0 * np.pi * np.arange(32) / 32
        cos_row, sin_row = np.zeros(LANES), np.zeros(LANES)
        if order < TOTAL // 4:
            cos_row[:96], sin_row[:96] = np.cos(order * low), np.sin(order * low)
        else:
            back = TOTAL // 2 - order
            cos_row[96:], sin_row[96:] = np.cos(back * high), -np.sin(back * high)
        return cos_row, sin_row
    angle = 2.0 * np.pi * ((np.arange(64) * (order - OWN * f)) % 64) / 64
    cos_row = 0.5 * np.concatenate([np.cos(angle), np.sin(angle)])
    sin_row = 0.5 * np.concatenate([np.sin(angle), -np.cos(angle)])
    return cos_row, sin_row


def pair_rows(f, order):
    cos_row, sin_row = wave_rows(f, order)
    return [(cos_row, -order * sin_row), (sin_row, order * cos_row)]


def top_row(f):
    row = np.zeros(LANES)
    if f == 0:
        row[96:] = 1.0
    else:
        angle = 2.0 * np.pi * ((np.arange(64) * (TOTAL // 2 - OWN * f)) % 64) / 64
        row[:] = np.concatenate([np.cos(angle), np.sin(angle)])
    return row


def forward_tables():
    tables = np.zeros((PEERS, 2 * LANES, 4 * LANES))

    def put(f, lane, rows):
        for parity in range(2):
            at = lane + parity
            tables[f, at, parity * LANES : (parity + 1) * LANES] = rows[0]
            tables[f, at, (2 + parity) * LANES : (3 + parity) * LANES] = rows[1]

    nothing = np.zeros(LANES)
    for f in range(PEERS):
        for m in range(OWN):
            if f == 0 and m == 0:
                put(f, 0, (wave_rows(0, 0)[0], nothing))
                put(f, 2, (top_row(0), nothing))
                continue
            for part, rows in enumerate(pair_rows(f, OWN * f + m)):
                put(f, 4 * m + 2 * part, rows)
        for m in range(REACH):
            left = (OWN * f - REACH + m) % (TOTAL // 2)
            for part, rows in enumerate(pair_rows(f, left)):
                put(f, LANES + 4 * m + 2 * part, rows)
            if f < PEERS - 1:
                for part, rows in enumerate(pair_rows(f, OWN * f + OWN + m)):
                    put(f, LANES + 32 + 4 * m + 2 * part, rows)
        if f == PEERS - 1:
            put(f, LANES + 32 + 2, (top_row(f), nothing))
            for m in range(1, REACH):
                order = TOTAL // 2 - REACH + m
                angle = 2.0 * np.pi * ((np.arange(64) * (TOTAL - order - OWN * f)) % 64) / 64
                cos_row = 0.5 * np.concatenate([np.cos(angle), np.sin(angle)])
                sin_row = 0.5 * np.concatenate([-np.sin(angle), np.cos(angle)])
                put(f, LANES + 64 + 4 * m, (cos_row, -order * sin_row))
                put(f, LANES + 64 + 4 * m + 2, (sin_row, order * cos_row))
    return tables


def inverse_tables():
    tables = np.zeros((PEERS, 4 * LANES, LANES))

    def put(f, lane, straight, turned):
        for parity in range(2):
            base = 2 * parity * LANES
            tables[f, base : base + LANES, lane + parity] = straight
            tables[f, base + LANES : base + 2 * LANES, lane + parity] = turned

    nothing = np.zeros(LANES)
    for f in range(PEERS):
        for m in range(OWN):
            order = OWN * f + m
            cos_row, sin_row = wave_rows(f, order)
            if f == 0:
                cos_row, sin_row = cos_row / 96, sin_row / 96
            else:
                cos_row, sin_row = cos_row / 32, sin_row / 32
            if order == 0:
                put(f, 0, cos_row, nothing)
                put(f, 2, top_row(0) / 32, nothing)
                continue
            put(f, 4 * m, cos_row, -order * sin_row)
            put(f, 4 * m + 2, sin_row, order * cos_row)
    return tables


def basis_lanes(low):
    if low:
        angles = np.concatenate(
            [2.0 * np.pi * np.arange(96) / 96, 2.0 * np.pi * np.arange(32) / 32]
        )
        share = np.concatenate([np.full(96, TOTAL / 96), np.full(32, TOTAL / 32)])
    else:
        angles = np.tile(2.0 * np.pi * np.arange(64) / 64, 2)
        share = np.full(LANES, TOTAL / 32)
    rows = [np.ones(LANES)]
    for order in range(1, REACH + 1):
        rows += [np.cos(order * angles), np.sin(order * angles)]
    return np.stack(rows), share


def moduli_tables():
    sampling = np.zeros((2, LANES, 7 * LANES))
    projection = np.zeros((2, 7 * LANES, LANES))
    for kind in range(2):
        rows, share = basis_lanes(kind == 0)
        for r in range(7):
            sampling[kind, 17 * r : 17 * r + 17, r * LANES : (r + 1) * LANES] = rows
            projection[kind, r * LANES : (r + 1) * LANES, 17 * r : 17 * r + 17] = (
                0.0001 * (rows * share).T
            )
    return sampling, projection


def in_two(table):
    table = np.asarray(table, np.float64)
    high = table.astype(ml_dtypes.bfloat16)
    low = (table - high.astype(np.float64)).astype(ml_dtypes.bfloat16)
    return high, low


def gll():
    x = np.array([-1.0, -math.sqrt(3.0 / 7.0), 0.0, math.sqrt(3.0 / 7.0), 1.0])
    weights = np.array([0.1, 49.0 / 90.0, 32.0 / 45.0, 49.0 / 90.0, 0.1])
    factor = [np.prod([x[i] - x[k] for k in range(5) if k != i]) for i in range(5)]
    derive = np.zeros((5, 5))
    for i in range(5):
        for k in range(5):
            if i != k:
                derive[i, k] = factor[i] / (factor[k] * (x[i] - x[k]))
            else:
                derive[i, k] = sum(1.0 / (x[i] - x[j]) for j in range(5) if j != i)
    return derive, np.outer(weights, weights).reshape(25)


DERIVE, WEIGHTS = gll()


def apply_line(matrix, x):
    m = matrix
    s0, s1 = x[0] + x[4], x[1] + x[3]
    d0, d1 = x[0] - x[4], x[1] - x[3]
    y = [None] * 5
    for i in range(2):
        even = (
            float(0.5 * (m[i, 0] + m[i, 4])) * s0
            + float(0.5 * (m[i, 1] + m[i, 3])) * s1
            + float(m[i, 2]) * x[2]
        )
        odd = float(0.5 * (m[i, 0] - m[i, 4])) * d0 + float(0.5 * (m[i, 1] - m[i, 3])) * d1
        y[i] = odd + even
        y[4 - i] = odd - even
    y[2] = float(m[2, 0]) * d0 + float(m[2, 1]) * d1
    return y


def halves(x):
    high = x.astype(bf16)
    return high, (x - high.astype(f32)).astype(bf16)


def product(x, high, low):
    x_high, x_low = halves(x)
    return (
        jnp.dot(x_high, high, preferred_element_type=f32)
        + jnp.dot(x_low, high, preferred_element_type=f32)
        + jnp.dot(x_high, low, preferred_element_type=f32)
    )


def voigt(v, w):
    v, w = min(v, w), max(v, w)
    return v * 6 - v * (v - 1) // 2 + w - v


def point_rows(ea, i, j):
    if 4 * ea + i == 8:
        return NEXT + j // 2, j % 2
    at = (4 * ea + i) * 33 + j
    return at // 2, at % 2


def spread_moduli_kernel(moduli_ref, out_ref):
    for t in range(3):
        block = moduli_ref[119 * t : 119 * t + 119, :]
        block = jnp.concatenate([block, jnp.zeros((LANES - 119, NODES), f32)], axis=0)
        turned = jnp.transpose(block)
        for e in range(PEERS):
            out_ref[e, t * NODES : t * NODES + NODES, :] = turned
    for e in range(PEERS):
        out_ref[e, 75:PART, :] = jnp.zeros((PART - 75, LANES), f32)


def pack_kernel(forward_ref, adjoint_ref, next_ref, x_ref, top_ref, low_ref):
    x_ref[0:3, 0:132, :] = forward_ref[...]
    x_ref[3:6, 0:132, :] = adjoint_ref[...]
    x_ref[:, 132:NEXT, :] = jnp.zeros((6, NEXT - 132, LANES), f32)
    x_ref[:, NEXT:ROWS, :] = next_ref[...]
    group = lax.broadcasted_iota(jnp.int32, (CHUNK, LANES), 1) // 32
    for c in range(6):
        low = x_ref[c, 0:CHUNK, :]
        top = pltpu.roll(low, 32, 1)
        for g in range(1, 4):
            rows = x_ref[c, CHUNK * g : CHUNK * g + CHUNK, :]
            low = jnp.where(group == g, pltpu.roll(rows, 32 * g, 1), low)
            top = jnp.where(
                group == g, rows if g == 3 else pltpu.roll(rows, 32 * g + 32, 1), top
            )
        low_ref[c] = low
        top_ref[c] = top


def strain_kernel(
    f_ref,
    x_ref,
    left_ref,
    right_ref,
    top_ref,
    wave_high,
    wave_low,
    project_high,
    project_low,
    radius_ref,
    weight_ref,
    strain_ref,
    terms_ref,
    halo_ref,
    sample_ref,
    central_ref,
    high_ref,
    low_ref,
    sum_ref,
):
    group = lax.broadcasted_iota(jnp.int32, (CHUNK, LANES), 1) // 32
    for c in range(6):
        left, right, top = left_ref[c], right_ref[c], top_ref[c]
        for g in range(4):
            a = left if g == 0 else pltpu.roll(left, (-32 * g) % LANES, 1)
            b = right if g == 1 else pltpu.roll(right, (32 - 32 * g) % LANES, 1)
            d = top if g == 2 else pltpu.roll(top, (64 - 32 * g) % LANES, 1)
            rows = jnp.where(group == 0, a, jnp.where(group == 1, b, d))
            halo_ref[c, CHUNK * g : CHUNK * g + CHUNK, :] = jnp.where(group == 3, 0.0, rows)
    for c in range(6):
        own = product(x_ref[c], wave_high[0, :LANES, :], wave_low[0, :LANES, :])
        beside = product(halo_ref[c], wave_high[0, LANES:, :], wave_low[0, LANES:, :])
        both = own + beside
        for k in range(4):
            sample_ref[c // 3, c % 3, k] = both[:, k * LANES : (k + 1) * LANES]
            if c < 3:
                sample_ref[2, c, k] = own[:, k * LANES : (k + 1) * LANES]

    @pl.loop(0, 3)
    def _(which):
        def strain_of(v):
            return strain_ref.at[which, v]

        for ea in range(2):

            def node(c, turned, i, j):
                row, parity = point_rows(ea, i, j)
                return sample_ref[which, c, 2 * turned + parity, pl.ds(row, 8, stride=2), :]

            def place(i, j):
                return pl.ds((i * 5 + j) * 16 + ea * 8, 8)

            def store(v, i, j, value, add):
                at = (which, v, place(i, j), slice(None))
                if add:
                    value = value + central_ref[at]
                central_ref[at] = value

            for c, v_a, v_b, v_p, add_a, add_b in (
                (0, 0, 5, 4, False, False),
                (1, 5, 1, 3, True, False),
                (2, 4, 3, 2, True, True),
            ):
                for i in range(5):
                    for j in range(5):
                        store(
                            v_p, i, j, radius_ref[place(i, j), :] * node(c, 1, i, j), False
                        )
                for j in range(5):
                    line = apply_line(DERIVE, [node(c, 0, i, j) for i in range(5)])
                    for i in range(5):
                        store(v_a, i, j, line[i], add_a)
                for i in range(5):
                    line = apply_line(DERIVE, [node(c, 0, i, j) for j in range(5)])
                    for j in range(5):
                        store(v_b, i, j, line[j], add_b)

    strain_ref[...] = central_ref[0:2]

    @pl.loop(0, NODES)
    def _(n):
        rows = pl.ds(pl.multiple_of(n * 16, 16), 16)
        a = [central_ref[1, v, rows, :] for v in range(6)]
        f = [central_ref[2, v, rows, :] * weight_ref[n] for v in range(6)]
        for v in range(6):
            for w in range(v, 6):
                term = f[v] * a[w]
                if v != w:
                    term = term + f[w] * a[v]
                r = voigt(v, w)
                high, low = halves(term)
                high_ref[rows, r * LANES : (r + 1) * LANES] = high
                low_ref[rows, r * LANES : (r + 1) * LANES] = low

    for t in range(3):
        cut = slice(t * 7 * LANES, (t + 1) * 7 * LANES)
        high, low = high_ref[:, cut], low_ref[:, cut]
        sum_ref[...] = (
            jnp.dot(high, project_high[0], preferred_element_type=f32)
            + jnp.dot(low, project_high[0], preferred_element_type=f32)
            + jnp.dot(high, project_low[0], preferred_element_type=f32)
        )
        for n in range(NODES):
            for ea in range(2):
                terms_ref[pl.ds(ea * 8 * PART + t * NODES + n, 8, stride=PART), :] = sum_ref[
                    n * 16 + ea * 8 : n * 16 + ea * 8 + 8, :
                ]
    for e in range(PEERS):
        terms_ref[e * PART + 75 : e * PART + PART, :] = jnp.zeros((PART - 75, LANES), f32)


def stress_kernel(
    f_ref,
    strain_ref,
    moduli_ref,
    sample_high,
    sample_low,
    back_high,
    back_low,
    radius_ref,
    weight_ref,
    forward_ref,
    forward_last_ref,
    adjoint_ref,
    adjoint_last_ref,
    mass_ref,
    forward_out,
    adjoint_out,
    edge_out,
    order_ref,
    moduli_s,
    stress_ref,
    line_ref,
    grid_ref,
):
    for t in range(3):
        for n in range(NODES):
            for ea in range(2):
                order_ref[n * 16 + ea * 8 : n * 16 + ea * 8 + 8, :] = (
                    moduli_ref[pl.ds(ea * 8 * PART + t * NODES + n, 8, stride=PART), :]
                    * float(WEIGHTS[n])
                )
        moduli_s[t] = product(order_ref[...], sample_high[0], sample_low[0])

    @pl.loop(0, NODES)
    def _(n):
        rows = pl.ds(pl.multiple_of(n * 16, 16), 16)
        for side in range(2):
            e = [strain_ref[side, v, rows, :] for v in range(6)]
            for v in range(6):
                total = None
                for w in range(6):
                    r = voigt(v, w)
                    term = (
                        moduli_s[r // 7, rows, (r % 7) * LANES : (r % 7 + 1) * LANES] * e[w]
                    )
                    total = term if total is None else total + term
                stress_ref[side, v, rows, :] = total

    grid_ref[...] = jnp.zeros(grid_ref.shape, f32)

    @pl.loop(0, 2)
    def _(side):
        for ea in range(2):

            def stress(v, i, j):
                return stress_ref[side, v, pl.ds((i * 5 + j) * 16 + ea * 8, 8), :]

            def add(c, turned, i, j, value):
                row, parity = point_rows(ea, i, j)
                at = (2 * parity + turned, side * 3 + c, pl.ds(row, 8, stride=2), slice(None))
                grid_ref[at] = grid_ref[at] + value

            for c, v_a, v_b, v_p in ((0, 0, 5, 4), (1, 5, 1, 3), (2, 4, 3, 2)):
                for j in range(5):
                    line = apply_line(DERIVE.T, [stress(v_a, i, j) for i in range(5)])
                    for i in range(5):
                        line_ref[i * 5 + j] = line[i]
                for i in range(5):
                    line = apply_line(DERIVE.T, [stress(v_b, i, j) for j in range(5)])
                    for j in range(5):
                        add(c, 0, i, j, line_ref[i * 5 + j] + line[j])
                for i in range(5):
                    for j in range(5):
                        at = pl.ds((i * 5 + j) * 16 + ea * 8, 8)
                        add(c, 1, i, j, radius_ref[at, :] * stress(v_p, i, j))

    for c in range(6):
        joined = jnp.concatenate([grid_ref[k, c] for k in range(4)], axis=1)
        force = product(joined, back_high[0], back_low[0])
        edge_out[c] = force[NEXT:ROWS, :]
        now_ref, last_ref, out_ref = (
            (forward_ref, forward_last_ref, forward_out)
            if c < 3
            else (adjoint_ref, adjoint_last_ref, adjoint_out)
        )
        out_ref[c % 3] = (
            2.0 * now_ref[c % 3] - last_ref[c % 3] - mass_ref[...] * force[0:132, :]
        )


def edge_kernel(forward_ref, adjoint_ref, edge_ref, mass_ref, forward_out, adjoint_out):
    forward_out[...] = forward_ref[...] - mass_ref[...] * edge_ref[0:3]
    adjoint_out[...] = adjoint_ref[...] - mass_ref[...] * edge_ref[3:6]


def collect_kernel(terms_ref, out_ref):
    total = terms_ref[0]
    for e in range(1, PEERS):
        total = total + terms_ref[e]
    for t in range(3):
        turned = jnp.transpose(total[t * NODES : t * NODES + NODES, :])
        out_ref[119 * t : 119 * t + 119, :] = turned[0:119, :]


def shape(*dims):
    return jax.ShapeDtypeStruct(dims, f32)


def whole(*dims):
    return pl.BlockSpec(dims, lambda i, f: (0,) * len(dims))


def picked(*dims):
    return pl.BlockSpec((1, *dims), lambda i, f: (f[0],) + (0,) * len(dims))


def kinded(*dims):
    return pl.BlockSpec(
        (1, *dims), lambda i, f: (jnp.minimum(f[0], 1),) + (0,) * len(dims)
    )


def scalars():
    return pl.BlockSpec(memory_space=pltpu.SMEM)


def params(mib):
    return pltpu.CompilerParams(vmem_limit_bytes=mib * 1024 * 1024)


def cost(us):
    return pl.CostEstimate(flops=int(us * 1e6), bytes_accessed=int(us * 3.0e6), transcendentals=0)


def body(forward_now, forward_last, adjoint_now, adjoint_last, moduli, inv_radius, inv_mass):
    f_at = lax.axis_index(FOURIER).astype(jnp.int32).reshape(1)
    slices = lax.axis_size(MERIDIAN)
    wave_high, wave_low = in_two(forward_tables())
    back_high, back_low = in_two(inverse_tables())
    sampling, projection = moduli_tables()
    sample_high, sample_low = in_two(sampling)
    project_high, project_low = in_two(projection)
    weights = jnp.asarray(WEIGHTS, f32)

    first_rows = jnp.concatenate([forward_now[:, :24], adjoint_now[:, :24]], axis=0)
    next_rows = lax.ppermute(first_rows, MERIDIAN, [(s, s - 1) for s in range(1, slices)])

    spread = pl.pallas_call(
        spread_moduli_kernel,
        out_shape=shape(PEERS, PART, LANES),
        compiler_params=params(8),
        cost_estimate=cost(2),
        name="spread",
    )(moduli.reshape(357, NODES))
    gathered = lax.all_to_all(spread, FOURIER, 0, 0, tiled=True).reshape(PEERS * PART, LANES)

    radius = jnp.broadcast_to(
        jnp.transpose(inv_radius.reshape(16, NODES)).reshape(400, 1), (400, LANES)
    )
    mass = jnp.tile(inv_mass.reshape(132, 2), (1, 64))

    x, top, low = pl.pallas_call(
        pack_kernel,
        out_shape=(shape(6, ROWS, LANES), shape(6, CHUNK, LANES), shape(6, CHUNK, LANES)),
        compiler_params=params(8),
        cost_estimate=cost(2),
        name="pack",
    )(forward_now, adjoint_now, next_rows)
    left = lax.ppermute(top, FOURIER, [(i, (i + 1) % PEERS) for i in range(PEERS)])
    right = lax.ppermute(low, FOURIER, [(i, (i - 1) % PEERS) for i in range(PEERS)])

    strain, terms = pl.pallas_call(
        strain_kernel,
        grid_spec=pltpu.PrefetchScalarGridSpec(
            num_scalar_prefetch=1,
            grid=(1,),
            in_specs=[
                whole(6, ROWS, LANES),
                whole(6, CHUNK, LANES),
                whole(6, CHUNK, LANES),
                whole(6, CHUNK, LANES),
                picked(2 * LANES, 4 * LANES),
                picked(2 * LANES, 4 * LANES),
                kinded(7 * LANES, LANES),
                kinded(7 * LANES, LANES),
                whole(400, LANES),
                scalars(),
            ],
            out_specs=(whole(2, 6, 400, LANES), whole(PEERS * PART, LANES)),
            scratch_shapes=[
                pltpu.VMEM((6, ROWS, LANES), f32),
                pltpu.VMEM((3, 3, 4, ROWS, LANES), f32),
                pltpu.VMEM((3, 6, 400, LANES), f32),
                pltpu.VMEM((400, 21 * LANES), bf16),
                pltpu.VMEM((400, 21 * LANES), bf16),
                pltpu.VMEM((400, LANES), f32),
            ],
        ),
        out_shape=(shape(2, 6, 400, LANES), shape(PEERS * PART, LANES)),
        compiler_params=params(40),
        cost_estimate=cost(8),
        name="strain",
    )(
        f_at, x, left, right, top, wave_high, wave_low, project_high, project_low, radius, weights
    )
    arrived = lax.all_to_all(
        terms.reshape(PEERS, PART, LANES), FOURIER, 0, 0, tiled=True
    )

    field = whole(3, 132, LANES)
    forward_part, adjoint_part, edge = pl.pallas_call(
        stress_kernel,
        grid_spec=pltpu.PrefetchScalarGridSpec(
            num_scalar_prefetch=1,
            grid=(1,),
            in_specs=[
                whole(2, 6, 400, LANES),
                whole(PEERS * PART, LANES),
                kinded(LANES, 7 * LANES),
                kinded(LANES, 7 * LANES),
                picked(4 * LANES, LANES),
                picked(4 * LANES, LANES),
                whole(400, LANES),
                scalars(),
                field,
                field,
                field,
                field,
                whole(132, LANES),
            ],
            out_specs=(field, field, whole(6, 24, LANES)),
            scratch_shapes=[
                pltpu.VMEM((400, LANES), f32),
                pltpu.VMEM((3, 400, 7 * LANES), f32),
                pltpu.VMEM((2, 6, 400, LANES), f32),
                pltpu.VMEM((NODES, 8, LANES), f32),
                pltpu.VMEM((4, 6, ROWS, LANES), f32),
            ],
        ),
        out_shape=(shape(3, 132, LANES), shape(3, 132, LANES), shape(6, 24, LANES)),
        compiler_params=params(40),
        cost_estimate=cost(8),
        name="stress",
    )(
        f_at, strain, gathered, sample_high, sample_low, back_high, back_low, radius, weights,
        forward_now, forward_last, adjoint_now, adjoint_last, mass,
    )
    carried = lax.ppermute(edge, MERIDIAN, [(s, s + 1) for s in range(slices - 1)])
    first = pl.BlockSpec((3, 24, LANES), lambda i: (0, 0, 0))
    forward_next, adjoint_next = pl.pallas_call(
        edge_kernel,
        grid=(1,),
        in_specs=[
            first,
            first,
            pl.BlockSpec((6, 24, LANES), lambda i: (0, 0, 0)),
            pl.BlockSpec((24, LANES), lambda i: (0, 0)),
        ],
        out_specs=(first, first),
        out_shape=(shape(3, 132, LANES), shape(3, 132, LANES)),
        input_output_aliases={0: 0, 1: 1},
        compiler_params=params(8),
        name="edge",
    )(forward_part, adjoint_part, carried, mass)
    kernel = pl.pallas_call(
        collect_kernel,
        out_shape=shape(357, NODES),
        compiler_params=params(8),
        name="collect",
    )(arrived)
    return forward_next, adjoint_next, kernel.reshape(21, 17, 1, NODES)


def solution(mesh):
    field = P(None, MERIDIAN, FOURIER)
    moduli = P(None, None, MERIDIAN, FOURIER)
    return jax.shard_map(
        body,
        mesh=mesh,
        in_specs=(field, field, field, field, moduli, P(MERIDIAN), P(MERIDIAN)),
        out_specs=(field, field, moduli),
        check_vma=False,
    )
```

```python
import math

import jax
import jax.numpy as jnp
import ml_dtypes
import numpy as np
from jax import lax
from jax.experimental import pallas as pl
from jax.experimental.pallas import tpu as pltpu
from jax.sharding import PartitionSpec as P

FOURIER = "fourier"
MERIDIAN = "meridian"
PEERS = 16
OWN = 32
REACH = 8
LANES = 128
TOTAL = 1024
ROWS = 160
NEXT = 136
CHUNK = 40
PART = 80
NODES = 25
LIMIT = 50 * 1024 * 1024

f32 = jnp.float32
bf16 = jnp.bfloat16


def wave_rows(f, order):
    if f == 0:
        low = 2.0 * np.pi * np.arange(96) / 96
        high = 2.0 * np.pi * np.arange(32) / 32
        cos_row, sin_row = np.zeros(LANES), np.zeros(LANES)
        if order < TOTAL // 4:
            cos_row[:96], sin_row[:96] = np.cos(order * low), np.sin(order * low)
        else:
            back = TOTAL // 2 - order
            cos_row[96:], sin_row[96:] = np.cos(back * high), -np.sin(back * high)
        return cos_row, sin_row
    angle = 2.0 * np.pi * ((np.arange(64) * (order - OWN * f)) % 64) / 64
    cos_row = 0.5 * np.concatenate([np.cos(angle), np.sin(angle)])
    sin_row = 0.5 * np.concatenate([np.sin(angle), -np.cos(angle)])
    return cos_row, sin_row


def pair_rows(f, order):
    cos_row, sin_row = wave_rows(f, order)
    return [(cos_row, -order * sin_row), (sin_row, order * cos_row)]


def top_row(f):
    row = np.zeros(LANES)
    if f == 0:
        row[96:] = 1.0
    else:
        angle = 2.0 * np.pi * ((np.arange(64) * (TOTAL // 2 - OWN * f)) % 64) / 64
        row[:] = np.concatenate([np.cos(angle), np.sin(angle)])
    return row


def forward_tables():
    tables = np.zeros((PEERS, 2 * LANES, 4 * LANES))

    def put(f, lane, rows):
        for parity in range(2):
            at = lane + parity
            tables[f, at, parity * LANES : (parity + 1) * LANES] = rows[0]
            tables[f, at, (2 + parity) * LANES : (3 + parity) * LANES] = rows[1]

    nothing = np.zeros(LANES)
    for f in range(PEERS):
        for m in range(OWN):
            if f == 0 and m == 0:
                put(f, 0, (wave_rows(0, 0)[0], nothing))
                put(f, 2, (top_row(0), nothing))
                continue
            for part, rows in enumerate(pair_rows(f, OWN * f + m)):
                put(f, 4 * m + 2 * part, rows)
        for m in range(REACH):
            left = (OWN * f - REACH + m) % (TOTAL // 2)
            for part, rows in enumerate(pair_rows(f, left)):
                put(f, LANES + 4 * m + 2 * part, rows)
            if f < PEERS - 1:
                for part, rows in enumerate(pair_rows(f, OWN * f + OWN + m)):
                    put(f, LANES + 32 + 4 * m + 2 * part, rows)
        if f == PEERS - 1:
            put(f, LANES + 32 + 2, (top_row(f), nothing))
            for m in range(1, REACH):
                order = TOTAL // 2 - REACH + m
                angle = 2.0 * np.pi * ((np.arange(64) * (TOTAL - order - OWN * f)) % 64) / 64
                cos_row = 0.5 * np.concatenate([np.cos(angle), np.sin(angle)])
                sin_row = 0.5 * np.concatenate([-np.sin(angle), np.cos(angle)])
                put(f, LANES + 64 + 4 * m, (cos_row, -order * sin_row))
                put(f, LANES + 64 + 4 * m + 2, (sin_row, order * cos_row))
    return tables


def inverse_tables():
    tables = np.zeros((PEERS, 4 * LANES, LANES))

    def put(f, lane, straight, turned):
        for parity in range(2):
            base = 2 * parity * LANES
            tables[f, base : base + LANES, lane + parity] = straight
            tables[f, base + LANES : base + 2 * LANES, lane + parity] = turned

    nothing = np.zeros(LANES)
    for f in range(PEERS):
        for m in range(OWN):
            order = OWN * f + m
            cos_row, sin_row = wave_rows(f, order)
            if f == 0:
                cos_row, sin_row = cos_row / 96, sin_row / 96
            else:
                cos_row, sin_row = cos_row / 32, sin_row / 32
            if order == 0:
                put(f, 0, cos_row, nothing)
                put(f, 2, top_row(0) / 32, nothing)
                continue
            put(f, 4 * m, cos_row, -order * sin_row)
            put(f, 4 * m + 2, sin_row, order * cos_row)
    return tables


def basis_lanes(low):
    if low:
        angles = np.concatenate(
            [2.0 * np.pi * np.arange(96) / 96, 2.0 * np.pi * np.arange(32) / 32]
        )
        share = np.concatenate([np.full(96, TOTAL / 96), np.full(32, TOTAL / 32)])
    else:
        angles = np.tile(2.0 * np.pi * np.arange(64) / 64, 2)
        share = np.full(LANES, TOTAL / 32)
    rows = [np.ones(LANES)]
    for order in range(1, REACH + 1):
        rows += [np.cos(order * angles), np.sin(order * angles)]
    return np.stack(rows), share


def moduli_tables():
    sampling = np.zeros((2, LANES, 7 * LANES))
    projection = np.zeros((2, 7 * LANES, LANES))
    for kind in range(2):
        rows, share = basis_lanes(kind == 0)
        for r in range(7):
            sampling[kind, 17 * r : 17 * r + 17, r * LANES : (r + 1) * LANES] = rows
            projection[kind, r * LANES : (r + 1) * LANES, 17 * r : 17 * r + 17] = (
                0.0001 * (rows * share).T
            )
    return sampling, projection


def in_two(table):
    table = np.asarray(table, np.float64)
    high = table.astype(ml_dtypes.bfloat16)
    low = (table - high.astype(np.float64)).astype(ml_dtypes.bfloat16)
    return high, low


BACK_ROWS = 2 * 4 * LANES
KIND_ROWS = 2 * 7 * LANES
PROJECT_AT = PEERS * BACK_ROWS
SAMPLE_AT = PROJECT_AT + 2 * KIND_ROWS


def narrow_tables():
    sampling, projection = moduli_tables()
    blocks = np.stack(np.split(sampling, 7, axis=2), axis=1)
    parts = [
        np.stack(in_two(table), axis=1).reshape(-1, LANES)
        for table in (inverse_tables(), projection, blocks)
    ]
    return np.concatenate(parts)


def table_rows(table_hbm, at, count):
    return table_hbm.at[pl.ds(pl.multiple_of(at, LANES), count), :]


def gll():
    x = np.array([-1.0, -math.sqrt(3.0 / 7.0), 0.0, math.sqrt(3.0 / 7.0), 1.0])
    weights = np.array([0.1, 49.0 / 90.0, 32.0 / 45.0, 49.0 / 90.0, 0.1])
    factor = [np.prod([x[i] - x[k] for k in range(5) if k != i]) for i in range(5)]
    derive = np.zeros((5, 5))
    for i in range(5):
        for k in range(5):
            if i != k:
                derive[i, k] = factor[i] / (factor[k] * (x[i] - x[k]))
            else:
                derive[i, k] = sum(1.0 / (x[i] - x[j]) for j in range(5) if j != i)
    return derive, np.outer(weights, weights).reshape(25)


DERIVE, WEIGHTS = gll()


def apply_line(matrix, x):
    m = matrix
    s0, s1 = x[0] + x[4], x[1] + x[3]
    d0, d1 = x[0] - x[4], x[1] - x[3]
    y = [None] * 5
    for i in range(2):
        even = (
            float(0.5 * (m[i, 0] + m[i, 4])) * s0
            + float(0.5 * (m[i, 1] + m[i, 3])) * s1
            + float(m[i, 2]) * x[2]
        )
        odd = float(0.5 * (m[i, 0] - m[i, 4])) * d0 + float(0.5 * (m[i, 1] - m[i, 3])) * d1
        y[i] = odd + even
        y[4 - i] = odd - even
    y[2] = float(m[2, 0]) * d0 + float(m[2, 1]) * d1
    return y


def halves(x):
    high = x.astype(bf16)
    return high, (x - high.astype(f32)).astype(bf16)


def product(x, high, low):
    x_high, x_low = halves(x)
    return (
        jnp.dot(x_high, high, preferred_element_type=f32)
        + jnp.dot(x_low, high, preferred_element_type=f32)
        + jnp.dot(x_high, low, preferred_element_type=f32)
    )


def voigt(v, w):
    v, w = min(v, w), max(v, w)
    return v * 6 - v * (v - 1) // 2 + w - v


def point_rows(ea, i, j):
    if 4 * ea + i == 8:
        return NEXT + j // 2, j % 2
    at = (4 * ea + i) * 33 + j
    return at // 2, at % 2


def started(sems, pairs):
    copies = [pltpu.make_async_copy(a, b, sems.at[n]) for n, (a, b) in enumerate(pairs)]
    for copy in copies:
        copy.start()
    return copies


def spread_kernel(moduli_hbm, spread_hbm, moduli_ref, part_ref, sems, out_sems):
    (moduli_copy,) = started(sems, ((moduli_hbm, moduli_ref),))
    part_ref[72:PART, :] = jnp.zeros((PART - 72, LANES), f32)
    moduli_copy.wait()
    for t in range(3):
        rows = [moduli_ref[7 * t + r, :, 0, :] for r in range(7)]
        block = jnp.concatenate(rows + [jnp.zeros((LANES - 119, NODES), f32)], axis=0)
        part_ref[t * NODES : t * NODES + NODES, :] = jnp.transpose(block)
    for copy in started(out_sems, [(part_ref, spread_hbm.at[e]) for e in range(PEERS)]):
        copy.wait()


def pack_kernel(
    now_hbm, next_hbm, far_hbm, near_hbm, top_hbm, x_ref, top_ref, low_ref, sems, out_sems
):
    copies = started(
        sems,
        (
            (now_hbm, x_ref.at[:, 0:132, :]),
            (next_hbm, x_ref.at[:, NEXT:ROWS, :]),
        ),
    )
    x_ref[:, 132:NEXT, :] = jnp.zeros((6, NEXT - 132, LANES), f32)
    for copy in copies:
        copy.wait()
    group = lax.broadcasted_iota(jnp.int32, (CHUNK, LANES), 1) // 32
    for c in range(6):
        low = x_ref[c, 0:CHUNK, :]
        top = pltpu.roll(low, 32, 1)
        for g in range(1, 4):
            rows = x_ref[c, CHUNK * g : CHUNK * g + CHUNK, :]
            low = jnp.where(group == g, pltpu.roll(rows, 32 * g, 1), low)
            top = jnp.where(
                group == g, rows if g == 3 else pltpu.roll(rows, 32 * g + 32, 1), top
            )
        low_ref[c] = low
        top_ref[c] = top
    odd = lax.rem(lax.axis_index(FOURIER), 2)
    (top_copy,) = started(out_sems, ((top_ref, top_hbm),))

    @pl.when(odd == 0)
    def _():
        far = pltpu.make_async_copy(low_ref, far_hbm, out_sems.at[1])
        near = pltpu.make_async_copy(top_ref, near_hbm, out_sems.at[2])
        far.start()
        near.start()
        far.wait()
        near.wait()

    @pl.when(odd == 1)
    def _():
        far = pltpu.make_async_copy(top_ref, far_hbm, out_sems.at[1])
        near = pltpu.make_async_copy(low_ref, near_hbm, out_sems.at[2])
        far.start()
        near.start()
        far.wait()
        near.wait()

    top_copy.wait()


def strain_kernel(
    now_hbm,
    next_hbm,
    far_hbm,
    near_hbm,
    top_hbm,
    wave_hbm,
    table_hbm,
    radius_hbm,
    strain_hbm,
    terms_hbm,
    x_ref,
    beside_ref,
    top_ref,
    wave,
    project,
    radius_ref,
    strain_ref,
    halo_ref,
    sample_ref,
    central_ref,
    high_ref,
    low_ref,
    sum_ref,
    terms_ref,
    sems,
    out_sems,
):
    f_at = lax.axis_index(FOURIER)
    copies = started(
        sems,
        (
            (far_hbm, beside_ref.at[lax.rem(f_at, 2)]),
            (near_hbm, beside_ref.at[1 - lax.rem(f_at, 2)]),
            (top_hbm, top_ref),
            (wave_hbm.at[f_at], wave),
            (now_hbm, x_ref.at[:, 0:132, :]),
            (next_hbm, x_ref.at[:, NEXT:ROWS, :]),
            (radius_hbm, radius_ref),
            (
                table_rows(table_hbm, PROJECT_AT + KIND_ROWS * jnp.minimum(f_at, 1), KIND_ROWS),
                project,
            ),
        ),
    )
    x_ref[:, 132:NEXT, :] = jnp.zeros((6, NEXT - 132, LANES), f32)
    for copy in copies[:3]:
        copy.wait()
    group = lax.broadcasted_iota(jnp.int32, (CHUNK, LANES), 1) // 32
    for c in range(6):
        left, right, top = beside_ref[0, c], beside_ref[1, c], top_ref[c]
        for g in range(4):
            a = left if g == 0 else pltpu.roll(left, (-32 * g) % LANES, 1)
            b = right if g == 1 else pltpu.roll(right, (32 - 32 * g) % LANES, 1)
            d = top if g == 2 else pltpu.roll(top, (64 - 32 * g) % LANES, 1)
            rows = jnp.where(group == 0, a, jnp.where(group == 1, b, d))
            halo_ref[c, CHUNK * g : CHUNK * g + CHUNK, :] = jnp.where(group == 3, 0.0, rows)
    for copy in copies[3:7]:
        copy.wait()
    radius_copy = pltpu.make_async_copy(radius_ref, strain_hbm.at[12], out_sems.at[2])
    radius_copy.start()
    for c in range(6):
        own = product(x_ref[c], wave[0, :LANES, :], wave[1, :LANES, :])
        beside = product(halo_ref[c], wave[0, LANES:, :], wave[1, LANES:, :])
        both = own + beside
        for k in range(4):
            sample_ref[c // 3, c % 3, k] = both[:, k * LANES : (k + 1) * LANES]
            if c < 3:
                sample_ref[2, c, k] = own[:, k * LANES : (k + 1) * LANES]

    def strains(which, out_ref, out_at):
        for ea in range(2):

            def node(c, turned, i, j):
                row, parity = point_rows(ea, i, j)
                return sample_ref[which, c, 2 * turned + parity, pl.ds(row, 8, stride=2), :]

            def place(i, j):
                return pl.ds((i * 5 + j) * 16 + ea * 8, 8)

            def store(v, i, j, value, add):
                at = (out_at + v, place(i, j), slice(None))
                if add:
                    value = value + out_ref[at]
                out_ref[at] = value

            for c, v_a, v_b, v_p, add_a, add_b in (
                (0, 0, 5, 4, False, False),
                (1, 5, 1, 3, True, False),
                (2, 4, 3, 2, True, True),
            ):
                for i in range(5):
                    for j in range(5):
                        store(
                            v_p, i, j, radius_ref[place(i, j), :] * node(c, 1, i, j), False
                        )
                for j in range(5):
                    line = apply_line(DERIVE, [node(c, 0, i, j) for i in range(5)])
                    for i in range(5):
                        store(v_a, i, j, line[i], add_a)
                for i in range(5):
                    line = apply_line(DERIVE, [node(c, 0, i, j) for j in range(5)])
                    for j in range(5):
                        store(v_b, i, j, line[j], add_b)

    @pl.loop(0, 2)
    def _(which):
        strains(which, strain_ref, which * 6)

    strain_copy = pltpu.make_async_copy(strain_ref, strain_hbm.at[0:12], out_sems.at[0])
    strain_copy.start()
    strains(2, central_ref, 0)

    @pl.loop(0, NODES)
    def _(n):
        rows = pl.ds(pl.multiple_of(n * 16, 16), 16)
        a = [strain_ref[6 + v, rows, :] for v in range(6)]
        f = [central_ref[v, rows, :] for v in range(6)]
        for v in range(6):
            for w in range(v, 6):
                term = f[v] * a[w]
                if v != w:
                    term = term + f[w] * a[v]
                r = voigt(v, w)
                high, low = halves(term)
                high_ref[rows, r * LANES : (r + 1) * LANES] = high
                low_ref[rows, r * LANES : (r + 1) * LANES] = low

    copies[7].wait()
    for t in range(3):
        cut = slice(t * 7 * LANES, (t + 1) * 7 * LANES)
        high, low = high_ref[:, cut], low_ref[:, cut]
        sum_ref[...] = (
            jnp.dot(high, project[: 7 * LANES, :], preferred_element_type=f32)
            + jnp.dot(low, project[: 7 * LANES, :], preferred_element_type=f32)
            + jnp.dot(high, project[7 * LANES :, :], preferred_element_type=f32)
        )
        for n in range(NODES):
            for ea in range(2):
                terms_ref[pl.ds(ea * 8 * PART + t * NODES + n, 8, stride=PART), :] = sum_ref[
                    n * 16 + ea * 8 : n * 16 + ea * 8 + 8, :
                ] * float(WEIGHTS[n])
    for e in range(PEERS):
        terms_ref[e * PART + 75 : e * PART + PART, :] = jnp.zeros((PART - 75, LANES), f32)
    terms_copy = pltpu.make_async_copy(terms_ref, terms_hbm, out_sems.at[1])
    terms_copy.start()
    strain_copy.wait()
    radius_copy.wait()
    terms_copy.wait()


def stress_kernel(
    moduli_hbm,
    table_hbm,
    strain_hbm,
    forward_hbm,
    adjoint_hbm,
    forward_last_hbm,
    adjoint_last_hbm,
    mass_hbm,
    forward_out,
    adjoint_out,
    edge_hbm,
    moduli_ref,
    sample,
    strain_ref,
    back,
    now_ref,
    last_ref,
    mass_ref,
    out_ref,
    edge_ref,
    order_ref,
    moduli_s,
    stress_ref,
    line_ref,
    grid_ref,
    sems,
    out_sems,
):
    f_at = lax.axis_index(FOURIER)
    copies = started(
        sems,
        (
            (moduli_hbm, moduli_ref),
            (
                table_rows(table_hbm, SAMPLE_AT + KIND_ROWS * jnp.minimum(f_at, 1), KIND_ROWS),
                sample,
            ),
            (strain_hbm, strain_ref),
            (table_rows(table_hbm, BACK_ROWS * f_at, BACK_ROWS), back),
            (forward_hbm, now_ref.at[0:3]),
            (adjoint_hbm, now_ref.at[3:6]),
            (forward_last_hbm, last_ref.at[0:3]),
            (adjoint_last_hbm, last_ref.at[3:6]),
            (mass_hbm, mass_ref),
        ),
    )
    grid_ref[...] = jnp.zeros(grid_ref.shape, f32)
    copies[0].wait()
    copies[1].wait()
    for t in range(3):
        for n in range(NODES):
            for ea in range(2):
                order_ref[n * 16 + ea * 8 : n * 16 + ea * 8 + 8, :] = (
                    moduli_ref[pl.ds(ea * 8 * PART + t * NODES + n, 8, stride=PART), :]
                    * float(WEIGHTS[n])
                )
        high, low = halves(order_ref[...])
        for r in range(7):
            at = r * LANES
            block = sample[at : at + LANES, :]
            rest = sample[7 * LANES + at : 8 * LANES + at, :]
            moduli_s[t, :, at : at + LANES] = (
                jnp.dot(high, block, preferred_element_type=f32)
                + jnp.dot(low, block, preferred_element_type=f32)
                + jnp.dot(high, rest, preferred_element_type=f32)
            )
    copies[2].wait()

    @pl.loop(0, NODES)
    def _(n):
        rows = pl.ds(pl.multiple_of(n * 16, 16), 16)
        for side in range(2):
            e = [strain_ref[side * 6 + v, rows, :] for v in range(6)]
            for v in range(6):
                total = None
                for w in range(6):
                    r = voigt(v, w)
                    term = (
                        moduli_s[r // 7, rows, (r % 7) * LANES : (r % 7 + 1) * LANES] * e[w]
                    )
                    total = term if total is None else total + term
                stress_ref[side, v, rows, :] = total

    @pl.loop(0, 2)
    def _(side):
        for ea in range(2):

            def stress(v, i, j):
                return stress_ref[side, v, pl.ds((i * 5 + j) * 16 + ea * 8, 8), :]

            def add(c, turned, i, j, value):
                row, parity = point_rows(ea, i, j)
                at = (2 * parity + turned, side * 3 + c, pl.ds(row, 8, stride=2), slice(None))
                grid_ref[at] = grid_ref[at] + value

            for c, v_a, v_b, v_p in ((0, 0, 5, 4), (1, 5, 1, 3), (2, 4, 3, 2)):
                for j in range(5):
                    line = apply_line(DERIVE.T, [stress(v_a, i, j) for i in range(5)])
                    for i in range(5):
                        line_ref[i * 5 + j] = line[i]
                for i in range(5):
                    line = apply_line(DERIVE.T, [stress(v_b, i, j) for j in range(5)])
                    for j in range(5):
                        add(c, 0, i, j, line_ref[i * 5 + j] + line[j])
                for i in range(5):
                    for j in range(5):
                        at = pl.ds((i * 5 + j) * 16 + ea * 8, 8)
                        add(c, 1, i, j, strain_ref[12, at, :] * stress(v_p, i, j))

    for copy in copies[3:]:
        copy.wait()
    mass = mass_ref[...]
    for c in range(6):
        joined = jnp.concatenate([grid_ref[k, c] for k in range(4)], axis=1)
        force = product(joined, back[: 4 * LANES, :], back[4 * LANES :, :])
        edge_ref[c] = force[NEXT:ROWS, :]
        out_ref[c] = 2.0 * now_ref[c] - last_ref[c] - mass * force[0:132, :]
    for copy in started(
        out_sems,
        (
            (edge_ref, edge_hbm),
            (out_ref.at[0:3], forward_out),
            (out_ref.at[3:6], adjoint_out),
        ),
    ):
        copy.wait()


def finish_kernel(
    forward_hbm,
    adjoint_hbm,
    edge_hbm,
    mass_hbm,
    terms_hbm,
    forward_out,
    adjoint_out,
    kernel_hbm,
    rows,
    edge_ref,
    mass_ref,
    terms_ref,
    kernel_ref,
    sems,
    out_sems,
):
    copies = started(
        sems,
        (
            (forward_hbm.at[:, 0:24, :], rows.at[0:3]),
            (adjoint_hbm.at[:, 0:24, :], rows.at[3:6]),
            (edge_hbm, edge_ref),
            (mass_hbm.at[0:24, :], mass_ref),
            (terms_hbm, terms_ref),
        ),
    )
    for copy in copies[:4]:
        copy.wait()
    mass = mass_ref[...]
    for c in range(6):
        rows[c] = rows[c] - mass * edge_ref[c]
    copies[4].wait()
    total = terms_ref[0]
    for e in range(1, PEERS):
        total = total + terms_ref[e]
    for t in range(3):
        turned = jnp.transpose(total[t * NODES : t * NODES + NODES, :])
        for r in range(7):
            kernel_ref[7 * t + r, :, 0, :] = turned[17 * r : 17 * r + 17, :]
    for copy in started(
        out_sems,
        (
            (rows.at[0:3], forward_out.at[:, 0:24, :]),
            (rows.at[3:6], adjoint_out.at[:, 0:24, :]),
            (kernel_ref, kernel_hbm),
        ),
    ):
        copy.wait()


def shape(*dims):
    return jax.ShapeDtypeStruct(dims, f32)


SMEM = pl.BlockSpec(memory_space=pltpu.SMEM)
HBM = pl.BlockSpec(memory_space=pltpu.HBM)
DMA = pltpu.SemaphoreType.DMA
VMEM = pltpu.VMEM


def call(kernel, name, us, ins, outs, scratch, aliases=None, limit=LIMIT):
    return pl.pallas_call(
        kernel,
        in_specs=ins,
        out_specs=(HBM,) * len(outs),
        out_shape=outs,
        scratch_shapes=scratch,
        input_output_aliases=aliases or {},
        compiler_params=pltpu.CompilerParams(vmem_limit_bytes=limit),
        cost_estimate=pl.CostEstimate(
            flops=int(us * 1e6), bytes_accessed=int(us * 3.0e6), transcendentals=0
        ),
        name=name,
    )


def swaps(first):
    route = []
    for i in range(first, PEERS + first, 2):
        route += [(i, (i + 1) % PEERS), ((i + 1) % PEERS, i)]
    return route


def body(forward_now, forward_last, adjoint_now, adjoint_last, moduli, inv_radius, inv_mass):
    slices = lax.axis_size(MERIDIAN)
    wave = np.stack(in_two(forward_tables()), axis=1)
    tables = narrow_tables()
    halo = (6, CHUNK, LANES)

    now = jnp.concatenate([forward_now, adjoint_now], axis=0)
    next_rows = lax.ppermute(now[:, :24], MERIDIAN, [(s, s - 1) for s in range(1, slices)])

    radius = jnp.broadcast_to(
        jnp.transpose(inv_radius.reshape(16, NODES)).reshape(400, 1), (400, LANES)
    )
    pair = inv_mass.reshape(132, 2)
    even = lax.broadcasted_iota(jnp.int32, (132, LANES), 1) % 2 == 0
    mass = jnp.where(even, pair[:, 0:1], pair[:, 1:2])

    spread = call(
        spread_kernel,
        "spread",
        4,
        [HBM],
        (shape(PEERS, PART, LANES),),
        [
            VMEM((21, 17, 1, NODES), f32),
            VMEM((PART, LANES), f32),
            DMA((1,)),
            DMA((PEERS,)),
        ],
        limit=62 * 1024 * 1024,
    )(moduli)[0]
    next_rows, spread, radius, mass = lax.optimization_barrier((next_rows, spread, radius, mass))
    far, near, top = call(
        pack_kernel,
        "pack",
        2,
        [HBM] * 2,
        (shape(*halo), shape(*halo), shape(*halo)),
        [VMEM((6, ROWS, LANES), f32), VMEM(halo, f32), VMEM(halo, f32), DMA((2,)), DMA((3,))],
    )(now, next_rows)
    far_in = lax.ppermute(far, FOURIER, swaps(1))
    near_in = lax.ppermute(near, FOURIER, swaps(0))
    spread, far_in, near_in = lax.optimization_barrier((spread, far_in, near_in))
    gathered = lax.all_to_all(spread, FOURIER, 0, 0, tiled=True).reshape(PEERS * PART, LANES)

    strain, terms = call(
        strain_kernel,
        "strain",
        8,
        [HBM] * 8,
        (shape(13, 400, LANES), shape(PEERS * PART, LANES)),
        [
            VMEM((6, ROWS, LANES), f32),
            VMEM((2, *halo), f32),
            VMEM(halo, f32),
            VMEM((2, 2 * LANES, 4 * LANES), bf16),
            VMEM((KIND_ROWS, LANES), bf16),
            VMEM((400, LANES), f32),
            VMEM((12, 400, LANES), f32),
            VMEM((6, ROWS, LANES), f32),
            VMEM((3, 3, 4, ROWS, LANES), f32),
            VMEM((6, 400, LANES), f32),
            VMEM((400, 21 * LANES), bf16),
            VMEM((400, 21 * LANES), bf16),
            VMEM((400, LANES), f32),
            VMEM((PEERS * PART, LANES), f32),
            DMA((8,)),
            DMA((3,)),
        ],
    )(now, next_rows, far_in, near_in, top, wave, tables, radius)
    arrived = lax.all_to_all(terms.reshape(PEERS, PART, LANES), FOURIER, 0, 0, tiled=True)

    forward_part, adjoint_part, edge = call(
        stress_kernel,
        "stress",
        8,
        [HBM] * 8,
        (shape(3, 132, LANES), shape(3, 132, LANES), shape(6, 24, LANES)),
        [
            VMEM((PEERS * PART, LANES), f32),
            VMEM((KIND_ROWS, LANES), bf16),
            VMEM((13, 400, LANES), f32),
            VMEM((BACK_ROWS, LANES), bf16),
            VMEM((6, 132, LANES), f32),
            VMEM((6, 132, LANES), f32),
            VMEM((132, LANES), f32),
            VMEM((6, 132, LANES), f32),
            VMEM((6, 24, LANES), f32),
            VMEM((400, LANES), f32),
            VMEM((3, 400, 7 * LANES), f32),
            VMEM((2, 6, 400, LANES), f32),
            VMEM((NODES, 8, LANES), f32),
            VMEM((4, 6, ROWS, LANES), f32),
            DMA((9,)),
            DMA((3,)),
        ],
        limit=62 * 1024 * 1024,
    )(
        gathered,
        tables,
        strain,
        forward_now,
        adjoint_now,
        forward_last,
        adjoint_last,
        mass,
    )
    carried = lax.ppermute(edge, MERIDIAN, [(s, s + 1) for s in range(slices - 1)])
    return call(
        finish_kernel,
        "finish",
        2,
        [HBM] * 5,
        (shape(3, 132, LANES), shape(3, 132, LANES), shape(21, 17, 1, NODES)),
        [
            VMEM((6, 24, LANES), f32),
            VMEM((6, 24, LANES), f32),
            VMEM((24, LANES), f32),
            VMEM((PEERS, PART, LANES), f32),
            VMEM((21, 17, 1, NODES), f32),
            DMA((5,)),
            DMA((3,)),
        ],
        {0: 0, 1: 1},
    )(forward_part, adjoint_part, carried, mass, arrived)


def solution(mesh):
    field = P(None, MERIDIAN, FOURIER)
    moduli = P(None, None, MERIDIAN, FOURIER)
    return jax.shard_map(
        body,
        mesh=mesh,
        in_specs=(field, field, field, field, moduli, P(MERIDIAN), P(MERIDIAN)),
        out_specs=(field, field, moduli),
        check_vma=False,
    )
```

```python
import math

import jax
import jax.numpy as jnp
import ml_dtypes
import numpy as np
from jax import lax
from jax.experimental import pallas as pl
from jax.experimental.pallas import tpu as pltpu
from jax.sharding import PartitionSpec as P

FOURIER = "fourier"
MERIDIAN = "meridian"
PEERS = 16
OWN = 32
REACH = 8
LANES = 128
TOTAL = 1024
ROWS = 160
NEXT = 136
CHUNK = 40
PART = 80
NODES = 25
LIMIT = 50 * 1024 * 1024

f32 = jnp.float32
bf16 = jnp.bfloat16


def wave_rows(f, order):
    if f == 0:
        low = 2.0 * np.pi * np.arange(96) / 96
        high = 2.0 * np.pi * np.arange(32) / 32
        cos_row, sin_row = np.zeros(LANES), np.zeros(LANES)
        if order < TOTAL // 4:
            cos_row[:96], sin_row[:96] = np.cos(order * low), np.sin(order * low)
        else:
            back = TOTAL // 2 - order
            cos_row[96:], sin_row[96:] = np.cos(back * high), -np.sin(back * high)
        return cos_row, sin_row
    angle = 2.0 * np.pi * ((np.arange(64) * (order - OWN * f)) % 64) / 64
    cos_row = 0.5 * np.concatenate([np.cos(angle), np.sin(angle)])
    sin_row = 0.5 * np.concatenate([np.sin(angle), -np.cos(angle)])
    return cos_row, sin_row


def pair_rows(f, order):
    cos_row, sin_row = wave_rows(f, order)
    return [(cos_row, -order * sin_row), (sin_row, order * cos_row)]


def top_row(f):
    row = np.zeros(LANES)
    if f == 0:
        row[96:] = 1.0
    else:
        angle = 2.0 * np.pi * ((np.arange(64) * (TOTAL // 2 - OWN * f)) % 64) / 64
        row[:] = np.concatenate([np.cos(angle), np.sin(angle)])
    return row


def forward_tables():
    tables = np.zeros((PEERS, 2 * LANES, 4 * LANES))

    def put(f, lane, rows):
        for parity in range(2):
            at = lane + parity
            tables[f, at, parity * LANES : (parity + 1) * LANES] = rows[0]
            tables[f, at, (2 + parity) * LANES : (3 + parity) * LANES] = rows[1]

    nothing = np.zeros(LANES)
    for f in range(PEERS):
        for m in range(OWN):
            if f == 0 and m == 0:
                put(f, 0, (wave_rows(0, 0)[0], nothing))
                put(f, 2, (top_row(0), nothing))
                continue
            for part, rows in enumerate(pair_rows(f, OWN * f + m)):
                put(f, 4 * m + 2 * part, rows)
        for m in range(REACH):
            left = (OWN * f - REACH + m) % (TOTAL // 2)
            for part, rows in enumerate(pair_rows(f, left)):
                put(f, LANES + 4 * m + 2 * part, rows)
            if f < PEERS - 1:
                for part, rows in enumerate(pair_rows(f, OWN * f + OWN + m)):
                    put(f, LANES + 32 + 4 * m + 2 * part, rows)
        if f == PEERS - 1:
            put(f, LANES + 32 + 2, (top_row(f), nothing))
            for m in range(1, REACH):
                order = TOTAL // 2 - REACH + m
                angle = 2.0 * np.pi * ((np.arange(64) * (TOTAL - order - OWN * f)) % 64) / 64
                cos_row = 0.5 * np.concatenate([np.cos(angle), np.sin(angle)])
                sin_row = 0.5 * np.concatenate([-np.sin(angle), np.cos(angle)])
                put(f, LANES + 64 + 4 * m, (cos_row, -order * sin_row))
                put(f, LANES + 64 + 4 * m + 2, (sin_row, order * cos_row))
    return tables


def inverse_tables():
    tables = np.zeros((PEERS, 4 * LANES, LANES))

    def put(f, lane, straight, turned):
        for parity in range(2):
            base = 2 * parity * LANES
            tables[f, base : base + LANES, lane + parity] = straight
            tables[f, base + LANES : base + 2 * LANES, lane + parity] = turned

    nothing = np.zeros(LANES)
    for f in range(PEERS):
        for m in range(OWN):
            order = OWN * f + m
            cos_row, sin_row = wave_rows(f, order)
            if f == 0:
                cos_row, sin_row = cos_row / 96, sin_row / 96
            else:
                cos_row, sin_row = cos_row / 32, sin_row / 32
            if order == 0:
                put(f, 0, cos_row, nothing)
                put(f, 2, top_row(0) / 32, nothing)
                continue
            put(f, 4 * m, cos_row, -order * sin_row)
            put(f, 4 * m + 2, sin_row, order * cos_row)
    return tables


def basis_lanes(low):
    if low:
        angles = np.concatenate(
            [2.0 * np.pi * np.arange(96) / 96, 2.0 * np.pi * np.arange(32) / 32]
        )
        share = np.concatenate([np.full(96, TOTAL / 96), np.full(32, TOTAL / 32)])
    else:
        angles = np.tile(2.0 * np.pi * np.arange(64) / 64, 2)
        share = np.full(LANES, TOTAL / 32)
    rows = [np.ones(LANES)]
    for order in range(1, REACH + 1):
        rows += [np.cos(order * angles), np.sin(order * angles)]
    return np.stack(rows), share


def moduli_tables():
    sampling = np.zeros((2, LANES, 7 * LANES))
    projection = np.zeros((2, 7 * LANES, LANES))
    for kind in range(2):
        rows, share = basis_lanes(kind == 0)
        for r in range(7):
            sampling[kind, 17 * r : 17 * r + 17, r * LANES : (r + 1) * LANES] = rows
            projection[kind, r * LANES : (r + 1) * LANES, 17 * r : 17 * r + 17] = (
                0.0001 * (rows * share).T
            )
    return sampling, projection


def in_two(table):
    table = np.asarray(table, np.float64)
    high = table.astype(ml_dtypes.bfloat16)
    low = (table - high.astype(np.float64)).astype(ml_dtypes.bfloat16)
    return high, low


BACK_ROWS = 2 * 4 * LANES
KIND_ROWS = 2 * 7 * LANES
PROJECT_AT = PEERS * BACK_ROWS


def narrow_tables(projection):
    parts = [
        np.stack(in_two(table), axis=1).reshape(-1, LANES)
        for table in (inverse_tables(), projection)
    ]
    return np.concatenate(parts)


def table_rows(table_hbm, at, count):
    return table_hbm.at[pl.ds(pl.multiple_of(at, LANES), count), :]


def gll():
    x = np.array([-1.0, -math.sqrt(3.0 / 7.0), 0.0, math.sqrt(3.0 / 7.0), 1.0])
    weights = np.array([0.1, 49.0 / 90.0, 32.0 / 45.0, 49.0 / 90.0, 0.1])
    factor = [np.prod([x[i] - x[k] for k in range(5) if k != i]) for i in range(5)]
    derive = np.zeros((5, 5))
    for i in range(5):
        for k in range(5):
            if i != k:
                derive[i, k] = factor[i] / (factor[k] * (x[i] - x[k]))
            else:
                derive[i, k] = sum(1.0 / (x[i] - x[j]) for j in range(5) if j != i)
    return derive, np.outer(weights, weights).reshape(25)


DERIVE, WEIGHTS = gll()


def apply_line(matrix, x):
    m = matrix
    s0, s1 = x[0] + x[4], x[1] + x[3]
    d0, d1 = x[0] - x[4], x[1] - x[3]
    y = [None] * 5
    for i in range(2):
        even = (
            float(0.5 * (m[i, 0] + m[i, 4])) * s0
            + float(0.5 * (m[i, 1] + m[i, 3])) * s1
            + float(m[i, 2]) * x[2]
        )
        odd = float(0.5 * (m[i, 0] - m[i, 4])) * d0 + float(0.5 * (m[i, 1] - m[i, 3])) * d1
        y[i] = odd + even
        y[4 - i] = odd - even
    y[2] = float(m[2, 0]) * d0 + float(m[2, 1]) * d1
    return y


def halves(x):
    high = x.astype(bf16)
    return high, (x - high.astype(f32)).astype(bf16)


def threes(x):
    high, low = halves(x)
    return jnp.concatenate([high, low, high], axis=1)


def beside(high, low, table):
    both = jnp.dot(high, table, preferred_element_type=f32)
    return (
        both[:, :LANES]
        + both[:, LANES:]
        + jnp.dot(low, table[:, :LANES], preferred_element_type=f32)
    )


def voigt(v, w):
    v, w = min(v, w), max(v, w)
    return v * 6 - v * (v - 1) // 2 + w - v


def point_rows(ea, i, j):
    if 4 * ea + i == 8:
        return NEXT + j // 2, j % 2
    at = (4 * ea + i) * 33 + j
    return at // 2, at % 2


def started(sems, pairs):
    copies = [pltpu.make_async_copy(a, b, sems.at[n]) for n, (a, b) in enumerate(pairs)]
    for copy in copies:
        copy.start()
    return copies


def spread_kernel(moduli_hbm, spread_hbm, moduli_ref, part_ref, sems, out_sems):
    (moduli_copy,) = started(sems, ((moduli_hbm, moduli_ref),))
    part_ref[72:PART, :] = jnp.zeros((PART - 72, LANES), f32)
    moduli_copy.wait()
    for t in range(3):
        rows = [moduli_ref[7 * t + r, :, 0, :] for r in range(7)]
        block = jnp.concatenate(rows + [jnp.zeros((LANES - 119, NODES), f32)], axis=0)
        part_ref[t * NODES : t * NODES + NODES, :] = jnp.transpose(block)
    for copy in started(out_sems, [(part_ref, spread_hbm.at[e]) for e in range(PEERS)]):
        copy.wait()


def pack_kernel(
    forward_hbm,
    adjoint_hbm,
    next_hbm,
    far_hbm,
    near_hbm,
    top_hbm,
    x_ref,
    top_ref,
    low_ref,
    sems,
    out_sems,
):
    copies = started(
        sems,
        (
            (forward_hbm, x_ref.at[0:3, 0:132, :]),
            (adjoint_hbm, x_ref.at[3:6, 0:132, :]),
            (next_hbm, x_ref.at[:, NEXT:ROWS, :]),
        ),
    )
    x_ref[:, 132:NEXT, :] = jnp.zeros((6, NEXT - 132, LANES), f32)
    for copy in copies:
        copy.wait()
    group = lax.broadcasted_iota(jnp.int32, (CHUNK, LANES), 1) // 32
    for c in range(6):
        low = x_ref[c, 0:CHUNK, :]
        top = pltpu.roll(low, 32, 1)
        for g in range(1, 4):
            rows = x_ref[c, CHUNK * g : CHUNK * g + CHUNK, :]
            low = jnp.where(group == g, pltpu.roll(rows, 32 * g, 1), low)
            top = jnp.where(
                group == g, rows if g == 3 else pltpu.roll(rows, 32 * g + 32, 1), top
            )
        low_ref[c] = low
        top_ref[c] = top
    odd = lax.rem(lax.axis_index(FOURIER), 2)
    (top_copy,) = started(out_sems, ((top_ref, top_hbm),))

    @pl.when(odd == 0)
    def _():
        far = pltpu.make_async_copy(low_ref, far_hbm, out_sems.at[1])
        near = pltpu.make_async_copy(top_ref, near_hbm, out_sems.at[2])
        far.start()
        near.start()
        far.wait()
        near.wait()

    @pl.when(odd == 1)
    def _():
        far = pltpu.make_async_copy(top_ref, far_hbm, out_sems.at[1])
        near = pltpu.make_async_copy(low_ref, near_hbm, out_sems.at[2])
        far.start()
        near.start()
        far.wait()
        near.wait()

    top_copy.wait()


def strains(sample_ref, which, radius_ref, out_ref, out_at):
    for ea in range(2):

        def node(c, turned, i, j):
            row, parity = point_rows(ea, i, j)
            return sample_ref[which, c, 2 * turned + parity, pl.ds(row, 8, stride=2), :]

        def place(i, j):
            return pl.ds((i * 5 + j) * 16 + ea * 8, 8)

        def store(v, i, j, value, add):
            at = (out_at + v, place(i, j), slice(None))
            if add:
                value = value + out_ref[at]
            out_ref[at] = value

        for c, v_a, v_b, v_p, add_a, add_b in (
            (0, 0, 5, 4, False, False),
            (1, 5, 1, 3, True, False),
            (2, 4, 3, 2, True, True),
        ):
            for i in range(5):
                for j in range(5):
                    store(
                        v_p, i, j, radius_ref[place(i, j), :] * node(c, 1, i, j), False
                    )
            for j in range(5):
                line = apply_line(DERIVE, [node(c, 0, i, j) for i in range(5)])
                for i in range(5):
                    store(v_a, i, j, line[i], add_a)
            for i in range(5):
                line = apply_line(DERIVE, [node(c, 0, i, j) for j in range(5)])
                for j in range(5):
                    store(v_b, i, j, line[j], add_b)


def strain_kernel(
    forward_hbm,
    adjoint_hbm,
    next_hbm,
    far_hbm,
    near_hbm,
    top_hbm,
    wave_hbm,
    table_hbm,
    radius_hbm,
    sample_hbm,
    strain_hbm,
    terms_hbm,
    x_ref,
    beside_ref,
    top_ref,
    wave,
    project,
    radius_ref,
    strain_ref,
    halo_ref,
    sample_ref,
    central_ref,
    high_ref,
    low_ref,
    sum_ref,
    terms_ref,
    sems,
    out_sems,
):
    f_at = lax.axis_index(FOURIER)
    copies = started(
        sems,
        (
            (far_hbm, beside_ref.at[lax.rem(f_at, 2)]),
            (near_hbm, beside_ref.at[1 - lax.rem(f_at, 2)]),
            (top_hbm, top_ref),
            (forward_hbm, x_ref.at[0:3, 0:132, :]),
            (adjoint_hbm, x_ref.at[3:6, 0:132, :]),
            (next_hbm, x_ref.at[:, NEXT:ROWS, :]),
            (radius_hbm, radius_ref),
        )
        + tuple(
            (wave_hbm.at[f_at, part], wave.at[k * LANES : (k + 1) * LANES, :])
            for k, part in enumerate((0, 0, 2, 1, 1, 3))
        )
        + tuple(
            (
                table_rows(
                    table_hbm,
                    PROJECT_AT + KIND_ROWS * jnp.minimum(f_at, 1) + 7 * LANES * k,
                    7 * LANES,
                ),
                project.at[:, k * LANES : (k + 1) * LANES],
            )
            for k in range(2)
        ),
    )
    x_ref[:, 132:NEXT, :] = jnp.zeros((6, NEXT - 132, LANES), f32)
    for copy in copies[:3]:
        copy.wait()
    group = lax.broadcasted_iota(jnp.int32, (CHUNK, LANES), 1) // 32
    for c in range(6):
        left, right, top = beside_ref[0, c], beside_ref[1, c], top_ref[c]
        for g in range(4):
            a = left if g == 0 else pltpu.roll(left, (-32 * g) % LANES, 1)
            b = right if g == 1 else pltpu.roll(right, (32 - 32 * g) % LANES, 1)
            d = top if g == 2 else pltpu.roll(top, (64 - 32 * g) % LANES, 1)
            rows = jnp.where(group == 0, a, jnp.where(group == 1, b, d))
            halo_ref[c, CHUNK * g : CHUNK * g + CHUNK, :] = jnp.where(group == 3, 0.0, rows)
    for copy in copies[3:13]:
        copy.wait()
    radius_copy = pltpu.make_async_copy(radius_ref, strain_hbm.at[6], out_sems.at[2])
    radius_copy.start()
    for c in range(6):
        own = jnp.dot(threes(x_ref[c]), wave[: 3 * LANES, :], preferred_element_type=f32)
        both = own + jnp.dot(
            threes(halo_ref[c]), wave[3 * LANES :, :], preferred_element_type=f32
        )
        for k in range(4):
            sample_ref[c // 3, c % 3, k] = both[:, k * LANES : (k + 1) * LANES]
            if c < 3:
                sample_ref[2, c, k] = own[:, k * LANES : (k + 1) * LANES]

    sample_copy = pltpu.make_async_copy(sample_ref.at[0], sample_hbm, out_sems.at[3])
    sample_copy.start()
    strains(sample_ref, 1, radius_ref, strain_ref, 0)
    strain_copy = pltpu.make_async_copy(strain_ref, strain_hbm.at[0:6], out_sems.at[0])
    strain_copy.start()
    strains(sample_ref, 2, radius_ref, central_ref, 0)

    @pl.loop(0, NODES)
    def _(n):
        rows = pl.ds(pl.multiple_of(n * 16, 16), 16)
        a = [strain_ref[v, rows, :] for v in range(6)]
        f = [central_ref[v, rows, :] for v in range(6)]
        for v in range(6):
            for w in range(v, 6):
                term = f[v] * a[w]
                if v != w:
                    term = term + f[w] * a[v]
                r = voigt(v, w)
                high, low = halves(term)
                high_ref[rows, r * LANES : (r + 1) * LANES] = high
                low_ref[rows, r * LANES : (r + 1) * LANES] = low

    copies[13].wait()
    copies[14].wait()
    for t in range(3):
        cut = slice(t * 7 * LANES, (t + 1) * 7 * LANES)
        high, low = high_ref[:, cut], low_ref[:, cut]
        sum_ref[...] = beside(high, low, project[...])
        for n in range(NODES):
            for ea in range(2):
                terms_ref[pl.ds(ea * 8 * PART + t * NODES + n, 8, stride=PART), :] = sum_ref[
                    n * 16 + ea * 8 : n * 16 + ea * 8 + 8, :
                ] * float(WEIGHTS[n])
    for e in range(PEERS):
        terms_ref[e * PART + 75 : e * PART + PART, :] = jnp.zeros((PART - 75, LANES), f32)
    terms_copy = pltpu.make_async_copy(terms_ref, terms_hbm, out_sems.at[1])
    terms_copy.start()
    sample_copy.wait()
    strain_copy.wait()
    radius_copy.wait()
    terms_copy.wait()


def stress_kernel(
    moduli_hbm,
    sample_hbm,
    table_hbm,
    forward_samples_hbm,
    strain_hbm,
    forward_hbm,
    adjoint_hbm,
    forward_last_hbm,
    adjoint_last_hbm,
    mass_hbm,
    forward_out,
    adjoint_out,
    edge_hbm,
    moduli_ref,
    sample,
    forward_samples,
    strain_ref,
    back,
    now_ref,
    last_ref,
    mass_ref,
    out_ref,
    edge_ref,
    order_ref,
    moduli_s,
    stress_ref,
    line_ref,
    grid_ref,
    sems,
    out_sems,
):
    f_at = lax.axis_index(FOURIER)
    kind = jnp.minimum(f_at, 1)
    copies = started(
        sems,
        (
            (moduli_hbm, moduli_ref),
            (sample_hbm.at[kind, 0], sample.at[0:LANES, :]),
            (sample_hbm.at[kind, 0], sample.at[LANES : 2 * LANES, :]),
            (sample_hbm.at[kind, 1], sample.at[2 * LANES :, :]),
            (forward_samples_hbm, forward_samples.at[0]),
            (strain_hbm, strain_ref.at[6:13]),
            (
                table_rows(table_hbm, BACK_ROWS * f_at, 4 * LANES),
                back.at[:, 0:LANES],
            ),
            (
                table_rows(table_hbm, BACK_ROWS * f_at + 4 * LANES, 4 * LANES),
                back.at[:, LANES : 2 * LANES],
            ),
            (forward_hbm, now_ref.at[0:3]),
            (adjoint_hbm, now_ref.at[3:6]),
            (forward_last_hbm, last_ref.at[0:3]),
            (adjoint_last_hbm, last_ref.at[3:6]),
            (mass_hbm, mass_ref),
        ),
    )
    grid_ref[...] = jnp.zeros(grid_ref.shape, f32)
    for copy in copies[:4]:
        copy.wait()
    for t in range(3):
        for n in range(NODES):
            for ea in range(2):
                order_ref[n * 16 + ea * 8 : n * 16 + ea * 8 + 8, :] = (
                    moduli_ref[pl.ds(ea * 8 * PART + t * NODES + n, 8, stride=PART), :]
                    * float(WEIGHTS[n])
                )
        moduli_s[t] = jnp.dot(
            threes(order_ref[...]), sample[...], preferred_element_type=f32
        )
    copies[4].wait()
    copies[5].wait()
    strains(forward_samples, 0, strain_ref.at[12], strain_ref, 0)

    @pl.loop(0, NODES)
    def _(n):
        rows = pl.ds(pl.multiple_of(n * 16, 16), 16)
        for side in range(2):
            e = [strain_ref[side * 6 + v, rows, :] for v in range(6)]
            for v in range(6):
                total = None
                for w in range(6):
                    r = voigt(v, w)
                    term = (
                        moduli_s[r // 7, rows, (r % 7) * LANES : (r % 7 + 1) * LANES] * e[w]
                    )
                    total = term if total is None else total + term
                stress_ref[side, v, rows, :] = total

    @pl.loop(0, 2)
    def _(side):
        for ea in range(2):

            def stress(v, i, j):
                return stress_ref[side, v, pl.ds((i * 5 + j) * 16 + ea * 8, 8), :]

            def add(c, turned, i, j, value):
                row, parity = point_rows(ea, i, j)
                at = (2 * parity + turned, side * 3 + c, pl.ds(row, 8, stride=2), slice(None))
                grid_ref[at] = grid_ref[at] + value

            for c, v_a, v_b, v_p in ((0, 0, 5, 4), (1, 5, 1, 3), (2, 4, 3, 2)):
                for j in range(5):
                    line = apply_line(DERIVE.T, [stress(v_a, i, j) for i in range(5)])
                    for i in range(5):
                        line_ref[i * 5 + j] = line[i]
                for i in range(5):
                    line = apply_line(DERIVE.T, [stress(v_b, i, j) for j in range(5)])
                    for j in range(5):
                        add(c, 0, i, j, line_ref[i * 5 + j] + line[j])
                for i in range(5):
                    for j in range(5):
                        at = pl.ds((i * 5 + j) * 16 + ea * 8, 8)
                        add(c, 1, i, j, strain_ref[12, at, :] * stress(v_p, i, j))

    for copy in copies[6:]:
        copy.wait()
    mass = mass_ref[...]
    for c in range(6):
        joined = jnp.concatenate([grid_ref[k, c] for k in range(4)], axis=1)
        force = beside(*halves(joined), back[...])
        edge_ref[c] = force[NEXT:ROWS, :]
        out_ref[c] = 2.0 * now_ref[c] - last_ref[c] - mass * force[0:132, :]
    for copy in started(
        out_sems,
        (
            (edge_ref, edge_hbm),
            (out_ref.at[0:3], forward_out),
            (out_ref.at[3:6], adjoint_out),
        ),
    ):
        copy.wait()


def finish_kernel(
    forward_hbm,
    adjoint_hbm,
    edge_hbm,
    mass_hbm,
    terms_hbm,
    forward_out,
    adjoint_out,
    kernel_hbm,
    rows,
    edge_ref,
    mass_ref,
    terms_ref,
    kernel_ref,
    sems,
    out_sems,
):
    copies = started(
        sems,
        (
            (forward_hbm.at[:, 0:24, :], rows.at[0:3]),
            (adjoint_hbm.at[:, 0:24, :], rows.at[3:6]),
            (edge_hbm, edge_ref),
            (mass_hbm.at[0:24, :], mass_ref),
            (terms_hbm, terms_ref),
        ),
    )
    for copy in copies[:4]:
        copy.wait()
    mass = mass_ref[...]
    for c in range(6):
        rows[c] = rows[c] - mass * edge_ref[c]
    copies[4].wait()
    total = terms_ref[0]
    for e in range(1, PEERS):
        total = total + terms_ref[e]
    for t in range(3):
        turned = jnp.transpose(total[t * NODES : t * NODES + NODES, :])
        for r in range(7):
            kernel_ref[7 * t + r, :, 0, :] = turned[17 * r : 17 * r + 17, :]
    for copy in started(
        out_sems,
        (
            (rows.at[0:3], forward_out.at[:, 0:24, :]),
            (rows.at[3:6], adjoint_out.at[:, 0:24, :]),
            (kernel_ref, kernel_hbm),
        ),
    ):
        copy.wait()


def shape(*dims):
    return jax.ShapeDtypeStruct(dims, f32)


SMEM = pl.BlockSpec(memory_space=pltpu.SMEM)
HBM = pl.BlockSpec(memory_space=pltpu.HBM)
DMA = pltpu.SemaphoreType.DMA
VMEM = pltpu.VMEM


def call(kernel, name, us, ins, outs, scratch, aliases=None, limit=LIMIT):
    return pl.pallas_call(
        kernel,
        in_specs=ins,
        out_specs=(HBM,) * len(outs),
        out_shape=outs,
        scratch_shapes=scratch,
        input_output_aliases=aliases or {},
        compiler_params=pltpu.CompilerParams(vmem_limit_bytes=limit),
        cost_estimate=pl.CostEstimate(
            flops=int(us * 1e6), bytes_accessed=int(us * 3.0e6), transcendentals=0
        ),
        name=name,
    )


def swaps(first):
    route = []
    for i in range(first, PEERS + first, 2):
        route += [(i, (i + 1) % PEERS), ((i + 1) % PEERS, i)]
    return route


def body(forward_now, forward_last, adjoint_now, adjoint_last, moduli, inv_radius, inv_mass):
    slices = lax.axis_size(MERIDIAN)
    wave = np.stack(in_two(forward_tables()), axis=1).reshape(PEERS, 4, LANES, 4 * LANES)
    sampling, projection = moduli_tables()
    sample = np.stack(in_two(sampling), axis=1)
    tables = narrow_tables(projection)
    halo = (6, CHUNK, LANES)

    first_rows = jnp.concatenate([forward_now[:, :24], adjoint_now[:, :24]], axis=0)
    moduli, first_rows = lax.optimization_barrier((moduli, first_rows))
    spread = call(
        spread_kernel,
        "spread",
        4,
        [HBM],
        (shape(PEERS, PART, LANES),),
        [
            VMEM((21, 17, 1, NODES), f32),
            VMEM((PART, LANES), f32),
            DMA((1,)),
            DMA((PEERS,)),
        ],
        limit=62 * 1024 * 1024,
    )(moduli)[0]
    gathered = lax.all_to_all(spread, FOURIER, 0, 0, tiled=True).reshape(PEERS * PART, LANES)
    next_rows = lax.ppermute(first_rows, MERIDIAN, [(s, s - 1) for s in range(1, slices)])

    pair = inv_mass.reshape(132, 2)
    even = lax.broadcasted_iota(jnp.int32, (132, LANES), 1) % 2 == 0
    mass = jnp.where(even, pair[:, 0:1], pair[:, 1:2])
    next_rows, mass = lax.optimization_barrier((next_rows, mass))
    far, near, top = call(
        pack_kernel,
        "pack",
        2,
        [HBM] * 3,
        (shape(*halo), shape(*halo), shape(*halo)),
        [VMEM((6, ROWS, LANES), f32), VMEM(halo, f32), VMEM(halo, f32), DMA((3,)), DMA((3,))],
        limit=62 * 1024 * 1024,
    )(forward_now, adjoint_now, next_rows)
    far_in = lax.ppermute(far, FOURIER, swaps(1))
    near_in = lax.ppermute(near, FOURIER, swaps(0))
    inv_radius, top = lax.optimization_barrier((inv_radius, top))
    radius = jnp.broadcast_to(
        jnp.transpose(inv_radius.reshape(16, NODES)).reshape(400, 1), (400, LANES)
    )
    radius, mass = lax.optimization_barrier((radius, mass))
    samples, strain, terms = call(
        strain_kernel,
        "strain",
        8,
        [HBM] * 9,
        (
            shape(3, 4, ROWS, LANES),
            shape(7, 400, LANES),
            shape(PEERS * PART, LANES),
        ),
        [
            VMEM((6, ROWS, LANES), f32),
            VMEM((2, *halo), f32),
            VMEM(halo, f32),
            VMEM((6 * LANES, 4 * LANES), bf16),
            VMEM((7 * LANES, 2 * LANES), bf16),
            VMEM((400, LANES), f32),
            VMEM((6, 400, LANES), f32),
            VMEM((6, ROWS, LANES), f32),
            VMEM((3, 3, 4, ROWS, LANES), f32),
            VMEM((6, 400, LANES), f32),
            VMEM((400, 21 * LANES), bf16),
            VMEM((400, 21 * LANES), bf16),
            VMEM((400, LANES), f32),
            VMEM((PEERS * PART, LANES), f32),
            DMA((15,)),
            DMA((4,)),
        ],
        limit=62 * 1024 * 1024,
    )(forward_now, adjoint_now, next_rows, far_in, near_in, top, wave, tables, radius)
    arrived = lax.all_to_all(terms.reshape(PEERS, PART, LANES), FOURIER, 0, 0, tiled=True)

    forward_part, adjoint_part, edge = call(
        stress_kernel,
        "stress",
        8,
        [HBM] * 10,
        (shape(3, 132, LANES), shape(3, 132, LANES), shape(6, 24, LANES)),
        [
            VMEM((PEERS * PART, LANES), f32),
            VMEM((3 * LANES, 7 * LANES), bf16),
            VMEM((1, 3, 4, ROWS, LANES), f32),
            VMEM((13, 400, LANES), f32),
            VMEM((4 * LANES, 2 * LANES), bf16),
            VMEM((6, 132, LANES), f32),
            VMEM((6, 132, LANES), f32),
            VMEM((132, LANES), f32),
            VMEM((6, 132, LANES), f32),
            VMEM((6, 24, LANES), f32),
            VMEM((400, LANES), f32),
            VMEM((3, 400, 7 * LANES), f32),
            VMEM((2, 6, 400, LANES), f32),
            VMEM((NODES, 8, LANES), f32),
            VMEM((4, 6, ROWS, LANES), f32),
            DMA((13,)),
            DMA((3,)),
        ],
        limit=62 * 1024 * 1024,
    )(
        gathered,
        sample,
        tables,
        samples,
        strain,
        forward_now,
        adjoint_now,
        forward_last,
        adjoint_last,
        mass,
    )
    carried = lax.ppermute(edge, MERIDIAN, [(s, s + 1) for s in range(slices - 1)])
    return call(
        finish_kernel,
        "finish",
        2,
        [HBM] * 5,
        (shape(3, 132, LANES), shape(3, 132, LANES), shape(21, 17, 1, NODES)),
        [
            VMEM((6, 24, LANES), f32),
            VMEM((6, 24, LANES), f32),
            VMEM((24, LANES), f32),
            VMEM((PEERS, PART, LANES), f32),
            VMEM((21, 17, 1, NODES), f32),
            DMA((5,)),
            DMA((3,)),
        ],
        {0: 0, 1: 1},
    )(forward_part, adjoint_part, carried, mass, arrived)


def solution(mesh):
    field = P(None, MERIDIAN, FOURIER)
    moduli = P(None, None, MERIDIAN, FOURIER)
    return jax.shard_map(
        body,
        mesh=mesh,
        in_specs=(field, field, field, field, moduli, P(MERIDIAN), P(MERIDIAN)),
        out_specs=(field, field, moduli),
        check_vma=False,
    )
```

```python
import math

import jax
import jax.numpy as jnp
import ml_dtypes
import numpy as np
from jax import lax
from jax.experimental import pallas as pl
from jax.experimental.pallas import tpu as pltpu
from jax.sharding import PartitionSpec as P

FOURIER = "fourier"
MERIDIAN = "meridian"
PEERS = 16
OWN = 32
REACH = 8
LANES = 128
TOTAL = 1024
ROWS = 160
NEXT = 136
CHUNK = 40
PART = 80
NODES = 25
LIMIT = 50 * 1024 * 1024

f32 = jnp.float32
bf16 = jnp.bfloat16


def wave_rows(f, order):
    if f == 0:
        low = 2.0 * np.pi * np.arange(96) / 96
        high = 2.0 * np.pi * np.arange(32) / 32
        cos_row, sin_row = np.zeros(LANES), np.zeros(LANES)
        if order < TOTAL // 4:
            cos_row[:96], sin_row[:96] = np.cos(order * low), np.sin(order * low)
        else:
            back = TOTAL // 2 - order
            cos_row[96:], sin_row[96:] = np.cos(back * high), -np.sin(back * high)
        return cos_row, sin_row
    angle = 2.0 * np.pi * ((np.arange(64) * (order - OWN * f)) % 64) / 64
    cos_row = 0.5 * np.concatenate([np.cos(angle), np.sin(angle)])
    sin_row = 0.5 * np.concatenate([np.sin(angle), -np.cos(angle)])
    return cos_row, sin_row


def pair_rows(f, order):
    cos_row, sin_row = wave_rows(f, order)
    return [(cos_row, -order * sin_row), (sin_row, order * cos_row)]


def top_row(f):
    row = np.zeros(LANES)
    if f == 0:
        row[96:] = 1.0
    else:
        angle = 2.0 * np.pi * ((np.arange(64) * (TOTAL // 2 - OWN * f)) % 64) / 64
        row[:] = np.concatenate([np.cos(angle), np.sin(angle)])
    return row


def forward_tables():
    tables = np.zeros((PEERS, 2 * LANES, 4 * LANES))

    def put(f, lane, rows):
        for parity in range(2):
            at = lane + parity
            tables[f, at, parity * LANES : (parity + 1) * LANES] = rows[0]
            tables[f, at, (2 + parity) * LANES : (3 + parity) * LANES] = rows[1]

    nothing = np.zeros(LANES)
    for f in range(PEERS):
        for m in range(OWN):
            if f == 0 and m == 0:
                put(f, 0, (wave_rows(0, 0)[0], nothing))
                put(f, 2, (top_row(0), nothing))
                continue
            for part, rows in enumerate(pair_rows(f, OWN * f + m)):
                put(f, 4 * m + 2 * part, rows)
        for m in range(REACH):
            left = (OWN * f - REACH + m) % (TOTAL // 2)
            for part, rows in enumerate(pair_rows(f, left)):
                put(f, LANES + 4 * m + 2 * part, rows)
            if f < PEERS - 1:
                for part, rows in enumerate(pair_rows(f, OWN * f + OWN + m)):
                    put(f, LANES + 32 + 4 * m + 2 * part, rows)
        if f == PEERS - 1:
            put(f, LANES + 32 + 2, (top_row(f), nothing))
            for m in range(1, REACH):
                order = TOTAL // 2 - REACH + m
                angle = 2.0 * np.pi * ((np.arange(64) * (TOTAL - order - OWN * f)) % 64) / 64
                cos_row = 0.5 * np.concatenate([np.cos(angle), np.sin(angle)])
                sin_row = 0.5 * np.concatenate([-np.sin(angle), np.cos(angle)])
                put(f, LANES + 64 + 4 * m, (cos_row, -order * sin_row))
                put(f, LANES + 64 + 4 * m + 2, (sin_row, order * cos_row))
    return tables


def inverse_tables():
    tables = np.zeros((PEERS, 4 * LANES, LANES))

    def put(f, lane, straight, turned):
        for parity in range(2):
            base = 2 * parity * LANES
            tables[f, base : base + LANES, lane + parity] = straight
            tables[f, base + LANES : base + 2 * LANES, lane + parity] = turned

    nothing = np.zeros(LANES)
    for f in range(PEERS):
        for m in range(OWN):
            order = OWN * f + m
            cos_row, sin_row = wave_rows(f, order)
            if f == 0:
                cos_row, sin_row = cos_row / 96, sin_row / 96
            else:
                cos_row, sin_row = cos_row / 32, sin_row / 32
            if order == 0:
                put(f, 0, cos_row, nothing)
                put(f, 2, top_row(0) / 32, nothing)
                continue
            put(f, 4 * m, cos_row, -order * sin_row)
            put(f, 4 * m + 2, sin_row, order * cos_row)
    return tables


def basis_lanes(low):
    if low:
        angles = np.concatenate(
            [2.0 * np.pi * np.arange(96) / 96, 2.0 * np.pi * np.arange(32) / 32]
        )
        share = np.concatenate([np.full(96, TOTAL / 96), np.full(32, TOTAL / 32)])
    else:
        angles = np.tile(2.0 * np.pi * np.arange(64) / 64, 2)
        share = np.full(LANES, TOTAL / 32)
    rows = [np.ones(LANES)]
    for order in range(1, REACH + 1):
        rows += [np.cos(order * angles), np.sin(order * angles)]
    return np.stack(rows), share


def moduli_tables():
    sampling = np.zeros((2, LANES, 7 * LANES))
    projection = np.zeros((2, 7 * LANES, LANES))
    for kind in range(2):
        rows, share = basis_lanes(kind == 0)
        for r in range(7):
            sampling[kind, 17 * r : 17 * r + 17, r * LANES : (r + 1) * LANES] = rows
            projection[kind, r * LANES : (r + 1) * LANES, 17 * r : 17 * r + 17] = (
                0.0001 * (rows * share).T
            )
    return sampling, projection


def in_two(table):
    table = np.asarray(table, np.float64)
    high = table.astype(ml_dtypes.bfloat16)
    low = (table - high.astype(np.float64)).astype(ml_dtypes.bfloat16)
    return high, low


BACK_ROWS = 2 * 4 * LANES
KIND_ROWS = 2 * 7 * LANES
PROJECT_AT = PEERS * BACK_ROWS


def narrow_tables(projection):
    parts = [
        np.stack(in_two(table), axis=1).reshape(-1, LANES)
        for table in (inverse_tables(), projection)
    ]
    return np.concatenate(parts)


def table_rows(table_hbm, at, count):
    return table_hbm.at[pl.ds(pl.multiple_of(at, LANES), count), :]


def gll():
    x = np.array([-1.0, -math.sqrt(3.0 / 7.0), 0.0, math.sqrt(3.0 / 7.0), 1.0])
    weights = np.array([0.1, 49.0 / 90.0, 32.0 / 45.0, 49.0 / 90.0, 0.1])
    factor = [np.prod([x[i] - x[k] for k in range(5) if k != i]) for i in range(5)]
    derive = np.zeros((5, 5))
    for i in range(5):
        for k in range(5):
            if i != k:
                derive[i, k] = factor[i] / (factor[k] * (x[i] - x[k]))
            else:
                derive[i, k] = sum(1.0 / (x[i] - x[j]) for j in range(5) if j != i)
    return derive, np.outer(weights, weights).reshape(25)


DERIVE, WEIGHTS = gll()


def apply_line(matrix, x):
    m = matrix
    s0, s1 = x[0] + x[4], x[1] + x[3]
    d0, d1 = x[0] - x[4], x[1] - x[3]
    y = [None] * 5
    for i in range(2):
        even = (
            float(0.5 * (m[i, 0] + m[i, 4])) * s0
            + float(0.5 * (m[i, 1] + m[i, 3])) * s1
            + float(m[i, 2]) * x[2]
        )
        odd = float(0.5 * (m[i, 0] - m[i, 4])) * d0 + float(0.5 * (m[i, 1] - m[i, 3])) * d1
        y[i] = odd + even
        y[4 - i] = odd - even
    y[2] = float(m[2, 0]) * d0 + float(m[2, 1]) * d1
    return y


def halves(x):
    high = x.astype(bf16)
    return high, (x - high.astype(f32)).astype(bf16)


def threes(x):
    high, low = halves(x)
    return jnp.concatenate([high, low, high], axis=1)


def beside(high, low, table):
    both = jnp.dot(high, table, preferred_element_type=f32)
    return (
        both[:, :LANES]
        + both[:, LANES:]
        + jnp.dot(low, table[:, :LANES], preferred_element_type=f32)
    )


def voigt(v, w):
    v, w = min(v, w), max(v, w)
    return v * 6 - v * (v - 1) // 2 + w - v


def point_rows(ea, i, j):
    if 4 * ea + i == 8:
        return NEXT + j // 2, j % 2
    at = (4 * ea + i) * 33 + j
    return at // 2, at % 2


def started(sems, pairs):
    copies = [pltpu.make_async_copy(a, b, sems.at[n]) for n, (a, b) in enumerate(pairs)]
    for copy in copies:
        copy.start()
    return copies


def radius_rows(line_ref):
    row = lax.broadcasted_iota(jnp.int32, (400, 400), 0)
    source = lax.broadcasted_iota(jnp.int32, (400, 400), 1)
    place = (row & 15) * NODES + lax.shift_right_logical(row, 4)
    chosen = jnp.where(place == source, line_ref[...][None, :], 0.0)
    return jnp.dot(
        chosen,
        jnp.ones((400, LANES), f32),
        precision=lax.Precision.HIGHEST,
        preferred_element_type=f32,
    )


def mass_rows(line_ref, rows):
    row = lax.broadcasted_iota(jnp.int32, (rows, 264), 0)
    source = lax.broadcasted_iota(jnp.int32, (rows, 264), 1)
    chosen = jnp.where(lax.shift_right_logical(source, 1) == row, line_ref[...][None, :], 0.0)
    parity = lax.broadcasted_iota(jnp.int32, (264, LANES), 0) & 1
    lane = lax.broadcasted_iota(jnp.int32, (264, LANES), 1) & 1
    return jnp.dot(
        chosen,
        jnp.where(parity == lane, 1.0, 0.0).astype(f32),
        precision=lax.Precision.HIGHEST,
        preferred_element_type=f32,
    )


def spread_kernel(moduli_hbm, spread_hbm, moduli_ref, part_ref, sems, out_sems):
    (moduli_copy,) = started(sems, ((moduli_hbm, moduli_ref),))
    part_ref[72:PART, :] = jnp.zeros((PART - 72, LANES), f32)
    moduli_copy.wait()
    for t in range(3):
        rows = [moduli_ref[7 * t + r, :, 0, :] for r in range(7)]
        block = jnp.concatenate(rows + [jnp.zeros((LANES - 119, NODES), f32)], axis=0)
        part_ref[t * NODES : t * NODES + NODES, :] = jnp.transpose(block)
    for copy in started(out_sems, [(part_ref, spread_hbm.at[e]) for e in range(PEERS)]):
        copy.wait()


def pack_kernel(
    forward_hbm,
    adjoint_hbm,
    next_hbm,
    far_hbm,
    near_hbm,
    top_hbm,
    x_ref,
    top_ref,
    low_ref,
    sems,
    out_sems,
):
    copies = started(
        sems,
        (
            (forward_hbm, x_ref.at[0:3, 0:132, :]),
            (adjoint_hbm, x_ref.at[3:6, 0:132, :]),
            (next_hbm, x_ref.at[:, NEXT:ROWS, :]),
        ),
    )
    x_ref[:, 132:NEXT, :] = jnp.zeros((6, NEXT - 132, LANES), f32)
    for copy in copies:
        copy.wait()
    group = lax.broadcasted_iota(jnp.int32, (CHUNK, LANES), 1) // 32
    for c in range(6):
        low = x_ref[c, 0:CHUNK, :]
        top = pltpu.roll(low, 32, 1)
        for g in range(1, 4):
            rows = x_ref[c, CHUNK * g : CHUNK * g + CHUNK, :]
            low = jnp.where(group == g, pltpu.roll(rows, 32 * g, 1), low)
            top = jnp.where(
                group == g, rows if g == 3 else pltpu.roll(rows, 32 * g + 32, 1), top
            )
        low_ref[c] = low
        top_ref[c] = top
    odd = lax.rem(lax.axis_index(FOURIER), 2)
    (top_copy,) = started(out_sems, ((top_ref, top_hbm),))

    @pl.when(odd == 0)
    def _():
        far = pltpu.make_async_copy(low_ref, far_hbm, out_sems.at[1])
        near = pltpu.make_async_copy(top_ref, near_hbm, out_sems.at[2])
        far.start()
        near.start()
        far.wait()
        near.wait()

    @pl.when(odd == 1)
    def _():
        far = pltpu.make_async_copy(top_ref, far_hbm, out_sems.at[1])
        near = pltpu.make_async_copy(low_ref, near_hbm, out_sems.at[2])
        far.start()
        near.start()
        far.wait()
        near.wait()

    top_copy.wait()


def strains(sample_ref, which, radius_ref, out_ref, out_at):
    for ea in range(2):

        def node(c, turned, i, j):
            row, parity = point_rows(ea, i, j)
            return sample_ref[which, c, 2 * turned + parity, pl.ds(row, 8, stride=2), :]

        def place(i, j):
            return pl.ds((i * 5 + j) * 16 + ea * 8, 8)

        def store(v, i, j, value, add):
            at = (out_at + v, place(i, j), slice(None))
            if add:
                value = value + out_ref[at]
            out_ref[at] = value

        for c, v_a, v_b, v_p, add_a, add_b in (
            (0, 0, 5, 4, False, False),
            (1, 5, 1, 3, True, False),
            (2, 4, 3, 2, True, True),
        ):
            for i in range(5):
                for j in range(5):
                    store(
                        v_p, i, j, radius_ref[place(i, j), :] * node(c, 1, i, j), False
                    )
            for j in range(5):
                line = apply_line(DERIVE, [node(c, 0, i, j) for i in range(5)])
                for i in range(5):
                    store(v_a, i, j, line[i], add_a)
            for i in range(5):
                line = apply_line(DERIVE, [node(c, 0, i, j) for j in range(5)])
                for j in range(5):
                    store(v_b, i, j, line[j], add_b)


def strain_kernel(
    forward_hbm,
    adjoint_hbm,
    next_hbm,
    far_hbm,
    near_hbm,
    top_hbm,
    wave_hbm,
    table_hbm,
    radius_hbm,
    sample_hbm,
    strain_hbm,
    terms_hbm,
    x_ref,
    beside_ref,
    top_ref,
    wave,
    project,
    radius_line,
    radius_ref,
    strain_ref,
    halo_ref,
    sample_ref,
    central_ref,
    high_ref,
    low_ref,
    sum_ref,
    terms_ref,
    sems,
    out_sems,
):
    f_at = lax.axis_index(FOURIER)
    copies = started(
        sems,
        (
            (far_hbm, beside_ref.at[lax.rem(f_at, 2)]),
            (near_hbm, beside_ref.at[1 - lax.rem(f_at, 2)]),
            (top_hbm, top_ref),
            (forward_hbm, x_ref.at[0:3, 0:132, :]),
            (adjoint_hbm, x_ref.at[3:6, 0:132, :]),
            (next_hbm, x_ref.at[:, NEXT:ROWS, :]),
            (radius_hbm, radius_line),
        )
        + tuple(
            (wave_hbm.at[f_at, part], wave.at[k * LANES : (k + 1) * LANES, :])
            for k, part in enumerate((0, 0, 2, 1, 1, 3))
        )
        + tuple(
            (
                table_rows(
                    table_hbm,
                    PROJECT_AT + KIND_ROWS * jnp.minimum(f_at, 1) + 7 * LANES * k,
                    7 * LANES,
                ),
                project.at[:, k * LANES : (k + 1) * LANES],
            )
            for k in range(2)
        ),
    )
    x_ref[:, 132:NEXT, :] = jnp.zeros((6, NEXT - 132, LANES), f32)
    copies[6].wait()
    radius_ref[...] = radius_rows(radius_line)
    for copy in copies[:3]:
        copy.wait()
    group = lax.broadcasted_iota(jnp.int32, (CHUNK, LANES), 1) // 32
    for c in range(6):
        left, right, top = beside_ref[0, c], beside_ref[1, c], top_ref[c]
        for g in range(4):
            a = left if g == 0 else pltpu.roll(left, (-32 * g) % LANES, 1)
            b = right if g == 1 else pltpu.roll(right, (32 - 32 * g) % LANES, 1)
            d = top if g == 2 else pltpu.roll(top, (64 - 32 * g) % LANES, 1)
            rows = jnp.where(group == 0, a, jnp.where(group == 1, b, d))
            halo_ref[c, CHUNK * g : CHUNK * g + CHUNK, :] = jnp.where(group == 3, 0.0, rows)
    for copy in copies[3:6] + copies[7:13]:
        copy.wait()
    radius_copy = pltpu.make_async_copy(radius_ref, strain_hbm.at[6], out_sems.at[2])
    radius_copy.start()
    for c in range(6):
        own = jnp.dot(threes(x_ref[c]), wave[: 3 * LANES, :], preferred_element_type=f32)
        both = own + jnp.dot(
            threes(halo_ref[c]), wave[3 * LANES :, :], preferred_element_type=f32
        )
        for k in range(4):
            sample_ref[c // 3, c % 3, k] = both[:, k * LANES : (k + 1) * LANES]
            if c < 3:
                sample_ref[2, c, k] = own[:, k * LANES : (k + 1) * LANES]

    sample_copy = pltpu.make_async_copy(sample_ref.at[0], sample_hbm, out_sems.at[3])
    sample_copy.start()
    strains(sample_ref, 1, radius_ref, strain_ref, 0)
    strain_copy = pltpu.make_async_copy(strain_ref, strain_hbm.at[0:6], out_sems.at[0])
    strain_copy.start()
    strains(sample_ref, 2, radius_ref, central_ref, 0)

    @pl.loop(0, NODES)
    def _(n):
        rows = pl.ds(pl.multiple_of(n * 16, 16), 16)
        a = [strain_ref[v, rows, :] for v in range(6)]
        f = [central_ref[v, rows, :] for v in range(6)]
        for v in range(6):
            for w in range(v, 6):
                term = f[v] * a[w]
                if v != w:
                    term = term + f[w] * a[v]
                r = voigt(v, w)
                high, low = halves(term)
                high_ref[rows, r * LANES : (r + 1) * LANES] = high
                low_ref[rows, r * LANES : (r + 1) * LANES] = low

    copies[13].wait()
    copies[14].wait()
    for t in range(3):
        cut = slice(t * 7 * LANES, (t + 1) * 7 * LANES)
        high, low = high_ref[:, cut], low_ref[:, cut]
        sum_ref[...] = beside(high, low, project[...])
        for n in range(NODES):
            for ea in range(2):
                terms_ref[pl.ds(ea * 8 * PART + t * NODES + n, 8, stride=PART), :] = sum_ref[
                    n * 16 + ea * 8 : n * 16 + ea * 8 + 8, :
                ] * float(WEIGHTS[n])
    for e in range(PEERS):
        terms_ref[e * PART + 75 : e * PART + PART, :] = jnp.zeros((PART - 75, LANES), f32)
    terms_copy = pltpu.make_async_copy(terms_ref, terms_hbm, out_sems.at[1])
    terms_copy.start()
    sample_copy.wait()
    strain_copy.wait()
    radius_copy.wait()
    terms_copy.wait()


def stress_kernel(
    moduli_hbm,
    sample_hbm,
    table_hbm,
    forward_samples_hbm,
    strain_hbm,
    forward_hbm,
    adjoint_hbm,
    forward_last_hbm,
    adjoint_last_hbm,
    mass_hbm,
    forward_out,
    adjoint_out,
    edge_hbm,
    moduli_ref,
    sample,
    forward_samples,
    strain_ref,
    back,
    now_ref,
    last_ref,
    mass_line,
    out_ref,
    edge_ref,
    order_ref,
    moduli_s,
    stress_ref,
    line_ref,
    grid_ref,
    sems,
    out_sems,
):
    f_at = lax.axis_index(FOURIER)
    kind = jnp.minimum(f_at, 1)
    copies = started(
        sems,
        (
            (moduli_hbm, moduli_ref),
            (sample_hbm.at[kind, 0], sample.at[0:LANES, :]),
            (sample_hbm.at[kind, 0], sample.at[LANES : 2 * LANES, :]),
            (sample_hbm.at[kind, 1], sample.at[2 * LANES :, :]),
            (forward_samples_hbm, forward_samples.at[0]),
            (strain_hbm, strain_ref.at[6:13]),
            (
                table_rows(table_hbm, BACK_ROWS * f_at, 4 * LANES),
                back.at[:, 0:LANES],
            ),
            (
                table_rows(table_hbm, BACK_ROWS * f_at + 4 * LANES, 4 * LANES),
                back.at[:, LANES : 2 * LANES],
            ),
            (forward_hbm, now_ref.at[0:3]),
            (adjoint_hbm, now_ref.at[3:6]),
            (forward_last_hbm, last_ref.at[0:3]),
            (adjoint_last_hbm, last_ref.at[3:6]),
            (mass_hbm, mass_line),
        ),
    )
    grid_ref[...] = jnp.zeros(grid_ref.shape, f32)
    for copy in copies[:4]:
        copy.wait()
    for t in range(3):
        for n in range(NODES):
            for ea in range(2):
                order_ref[n * 16 + ea * 8 : n * 16 + ea * 8 + 8, :] = (
                    moduli_ref[pl.ds(ea * 8 * PART + t * NODES + n, 8, stride=PART), :]
                    * float(WEIGHTS[n])
                )
        moduli_s[t] = jnp.dot(
            threes(order_ref[...]), sample[...], preferred_element_type=f32
        )
    copies[4].wait()
    copies[5].wait()
    strains(forward_samples, 0, strain_ref.at[12], strain_ref, 0)

    @pl.loop(0, NODES)
    def _(n):
        rows = pl.ds(pl.multiple_of(n * 16, 16), 16)
        for side in range(2):
            e = [strain_ref[side * 6 + v, rows, :] for v in range(6)]
            for v in range(6):
                total = None
                for w in range(6):
                    r = voigt(v, w)
                    term = (
                        moduli_s[r // 7, rows, (r % 7) * LANES : (r % 7 + 1) * LANES] * e[w]
                    )
                    total = term if total is None else total + term
                stress_ref[side, v, rows, :] = total

    @pl.loop(0, 2)
    def _(side):
        for ea in range(2):

            def stress(v, i, j):
                return stress_ref[side, v, pl.ds((i * 5 + j) * 16 + ea * 8, 8), :]

            def add(c, turned, i, j, value):
                row, parity = point_rows(ea, i, j)
                at = (2 * parity + turned, side * 3 + c, pl.ds(row, 8, stride=2), slice(None))
                grid_ref[at] = grid_ref[at] + value

            for c, v_a, v_b, v_p in ((0, 0, 5, 4), (1, 5, 1, 3), (2, 4, 3, 2)):
                for j in range(5):
                    line = apply_line(DERIVE.T, [stress(v_a, i, j) for i in range(5)])
                    for i in range(5):
                        line_ref[i * 5 + j] = line[i]
                for i in range(5):
                    line = apply_line(DERIVE.T, [stress(v_b, i, j) for j in range(5)])
                    for j in range(5):
                        add(c, 0, i, j, line_ref[i * 5 + j] + line[j])
                for i in range(5):
                    for j in range(5):
                        at = pl.ds((i * 5 + j) * 16 + ea * 8, 8)
                        add(c, 1, i, j, strain_ref[12, at, :] * stress(v_p, i, j))

    for copy in copies[6:]:
        copy.wait()
    mass = mass_rows(mass_line, 132)
    for c in range(6):
        joined = jnp.concatenate([grid_ref[k, c] for k in range(4)], axis=1)
        force = beside(*halves(joined), back[...])
        edge_ref[c] = force[NEXT:ROWS, :]
        out_ref[c] = 2.0 * now_ref[c] - last_ref[c] - mass * force[0:132, :]
    for copy in started(
        out_sems,
        (
            (edge_ref, edge_hbm),
            (out_ref.at[0:3], forward_out),
            (out_ref.at[3:6], adjoint_out),
        ),
    ):
        copy.wait()


def finish_kernel(
    forward_hbm,
    adjoint_hbm,
    edge_hbm,
    mass_hbm,
    terms_hbm,
    forward_out,
    adjoint_out,
    kernel_hbm,
    rows,
    edge_ref,
    mass_line,
    terms_ref,
    kernel_ref,
    sems,
    out_sems,
):
    copies = started(
        sems,
        (
            (forward_hbm.at[:, 0:24, :], rows.at[0:3]),
            (adjoint_hbm.at[:, 0:24, :], rows.at[3:6]),
            (edge_hbm, edge_ref),
            (mass_hbm, mass_line),
            (terms_hbm, terms_ref),
        ),
    )
    for copy in copies[:4]:
        copy.wait()
    mass = mass_rows(mass_line, 24)
    for c in range(6):
        rows[c] = rows[c] - mass * edge_ref[c]
    copies[4].wait()
    total = terms_ref[0]
    for e in range(1, PEERS):
        total = total + terms_ref[e]
    for t in range(3):
        turned = jnp.transpose(total[t * NODES : t * NODES + NODES, :])
        for r in range(7):
            kernel_ref[7 * t + r, :, 0, :] = turned[17 * r : 17 * r + 17, :]
    for copy in started(
        out_sems,
        (
            (rows.at[0:3], forward_out.at[:, 0:24, :]),
            (rows.at[3:6], adjoint_out.at[:, 0:24, :]),
            (kernel_ref, kernel_hbm),
        ),
    ):
        copy.wait()


def shape(*dims):
    return jax.ShapeDtypeStruct(dims, f32)


SMEM = pl.BlockSpec(memory_space=pltpu.SMEM)
HBM = pl.BlockSpec(memory_space=pltpu.HBM)
DMA = pltpu.SemaphoreType.DMA
VMEM = pltpu.VMEM


def call(kernel, name, us, ins, outs, scratch, aliases=None, limit=LIMIT):
    return pl.pallas_call(
        kernel,
        in_specs=ins,
        out_specs=(HBM,) * len(outs),
        out_shape=outs,
        scratch_shapes=scratch,
        input_output_aliases=aliases or {},
        compiler_params=pltpu.CompilerParams(vmem_limit_bytes=limit),
        cost_estimate=pl.CostEstimate(
            flops=int(us * 1e6), bytes_accessed=int(us * 3.0e6), transcendentals=0
        ),
        name=name,
    )


def swaps(first):
    route = []
    for i in range(first, PEERS + first, 2):
        route += [(i, (i + 1) % PEERS), ((i + 1) % PEERS, i)]
    return route


def body(forward_now, forward_last, adjoint_now, adjoint_last, moduli, inv_radius, inv_mass):
    slices = lax.axis_size(MERIDIAN)
    wave = np.stack(in_two(forward_tables()), axis=1).reshape(PEERS, 4, LANES, 4 * LANES)
    sampling, projection = moduli_tables()
    sample = np.stack(in_two(sampling), axis=1)
    tables = narrow_tables(projection)
    halo = (6, CHUNK, LANES)

    first_rows = jnp.concatenate([forward_now[:, :24], adjoint_now[:, :24]], axis=0)
    moduli, first_rows = lax.optimization_barrier((moduli, first_rows))
    spread = call(
        spread_kernel,
        "spread",
        4,
        [HBM],
        (shape(PEERS, PART, LANES),),
        [
            VMEM((21, 17, 1, NODES), f32),
            VMEM((PART, LANES), f32),
            DMA((1,)),
            DMA((PEERS,)),
        ],
        limit=62 * 1024 * 1024,
    )(moduli)[0]
    next_rows = lax.ppermute(first_rows, MERIDIAN, [(s, s - 1) for s in range(1, slices)])
    spread, next_rows = lax.optimization_barrier((spread, next_rows))
    gathered = lax.all_to_all(spread, FOURIER, 0, 0, tiled=True).reshape(PEERS * PART, LANES)

    far, near, top = call(
        pack_kernel,
        "pack",
        2,
        [HBM] * 3,
        (shape(*halo), shape(*halo), shape(*halo)),
        [VMEM((6, ROWS, LANES), f32), VMEM(halo, f32), VMEM(halo, f32), DMA((3,)), DMA((3,))],
        limit=62 * 1024 * 1024,
    )(forward_now, adjoint_now, next_rows)
    far_in = lax.ppermute(far, FOURIER, swaps(1))
    near_in = lax.ppermute(near, FOURIER, swaps(0))
    samples, strain, terms = call(
        strain_kernel,
        "strain",
        8,
        [HBM] * 9,
        (
            shape(3, 4, ROWS, LANES),
            shape(7, 400, LANES),
            shape(PEERS * PART, LANES),
        ),
        [
            VMEM((6, ROWS, LANES), f32),
            VMEM((2, *halo), f32),
            VMEM(halo, f32),
            VMEM((6 * LANES, 4 * LANES), bf16),
            VMEM((7 * LANES, 2 * LANES), bf16),
            VMEM((400,), f32),
            VMEM((400, LANES), f32),
            VMEM((6, 400, LANES), f32),
            VMEM((6, ROWS, LANES), f32),
            VMEM((3, 3, 4, ROWS, LANES), f32),
            VMEM((6, 400, LANES), f32),
            VMEM((400, 21 * LANES), bf16),
            VMEM((400, 21 * LANES), bf16),
            VMEM((400, LANES), f32),
            VMEM((PEERS * PART, LANES), f32),
            DMA((15,)),
            DMA((4,)),
        ],
        limit=62 * 1024 * 1024,
    )(forward_now, adjoint_now, next_rows, far_in, near_in, top, wave, tables, inv_radius)
    arrived = lax.all_to_all(terms.reshape(PEERS, PART, LANES), FOURIER, 0, 0, tiled=True)

    forward_part, adjoint_part, edge = call(
        stress_kernel,
        "stress",
        8,
        [HBM] * 10,
        (shape(3, 132, LANES), shape(3, 132, LANES), shape(6, 24, LANES)),
        [
            VMEM((PEERS * PART, LANES), f32),
            VMEM((3 * LANES, 7 * LANES), bf16),
            VMEM((1, 3, 4, ROWS, LANES), f32),
            VMEM((13, 400, LANES), f32),
            VMEM((4 * LANES, 2 * LANES), bf16),
            VMEM((6, 132, LANES), f32),
            VMEM((6, 132, LANES), f32),
            VMEM((264,), f32),
            VMEM((6, 132, LANES), f32),
            VMEM((6, 24, LANES), f32),
            VMEM((400, LANES), f32),
            VMEM((3, 400, 7 * LANES), f32),
            VMEM((2, 6, 400, LANES), f32),
            VMEM((NODES, 8, LANES), f32),
            VMEM((4, 6, ROWS, LANES), f32),
            DMA((13,)),
            DMA((3,)),
        ],
        limit=62 * 1024 * 1024,
    )(
        gathered,
        sample,
        tables,
        samples,
        strain,
        forward_now,
        adjoint_now,
        forward_last,
        adjoint_last,
        inv_mass,
    )
    carried = lax.ppermute(edge, MERIDIAN, [(s, s + 1) for s in range(slices - 1)])
    return call(
        finish_kernel,
        "finish",
        2,
        [HBM] * 5,
        (shape(3, 132, LANES), shape(3, 132, LANES), shape(21, 17, 1, NODES)),
        [
            VMEM((6, 24, LANES), f32),
            VMEM((6, 24, LANES), f32),
            VMEM((264,), f32),
            VMEM((PEERS, PART, LANES), f32),
            VMEM((21, 17, 1, NODES), f32),
            DMA((5,)),
            DMA((3,)),
        ],
        {0: 0, 1: 1},
    )(forward_part, adjoint_part, carried, inv_mass, arrived)


def solution(mesh):
    field = P(None, MERIDIAN, FOURIER)
    moduli = P(None, None, MERIDIAN, FOURIER)
    return jax.shard_map(
        body,
        mesh=mesh,
        in_specs=(field, field, field, field, moduli, P(MERIDIAN), P(MERIDIAN)),
        out_specs=(field, field, moduli),
        check_vma=False,
    )
```
